256 devices in a mesh: row: 32 (over x, z), col: 8 (over y, core).
Axes of the slice: x: 4, y: 4, z: 8, core: 2. Of those that a mesh axis runs over, the one named last changes fastest.
Arguments:
- node_latents: bfloat16 [20480, 512], P(('col', 'row')), may hold values from -6 to 6
- edge_latents: bfloat16 [32, 8, 1024, 512], P('row', 'col'), may hold values from -6 to 6
- cotangent: bfloat16 [32, 8, 1024, 512], P('row', 'col'), may hold values from -6 to 6
- senders: int32 [32, 8, 1024], P('row', 'col'), may hold values from 0 to 2559, as said below
- receivers: int32 [32, 8, 1024], P('row', 'col'), may hold values from 0 to 639
- edge_count: int32 [32, 8], P('row', 'col'), may hold values from 512 to 1024, as said below
- w1: bfloat16 [1536, 512], replicated, may hold values from -0.15625 to 0.15625
- b1: float32 [512], replicated, may hold values from -4 to 4
- w2: bfloat16 [512, 512], replicated, may hold values from -0.25 to 0.25
- b2: float32 [512], replicated, may hold values from -4 to 4
- gamma: float32 [512], replicated, may hold values from 0.5 to 2
Outputs:
- grad_edges: bfloat16 [32, 8, 1024, 512], P('row', 'col')
- grad_nodes: float32 [20480, 512], P(('col', 'row'))
- grad_w1: float32 [1536, 512], replicated
- grad_b1: float32 [512], replicated
- grad_w2: float32 [512, 512], replicated
- grad_b2: float32 [512], replicated
- grad_gamma: float32 [512], replicated
The draws below stay inside these ranges and needn't reach their ends.
Inputs may be any that keep to these rules, and one draw needn't show every extreme that they name: `edge_count`: a multiple of 128; 1024 in at least one block of every draw. Among the 1024 slots of one block, at most 64 have senders in one range o * 80 to o * 80 + 79; in every block of a column of blocks the same range holds exactly 64 of them.
All inputs are finite; a program needn't handle non-finite values.
Results may differ from the reference program's by a relative error of at most 0.015.
Values may be sent and summed in bfloat16 or wider, within the bound.
No kernel may reach another device: no remote copies, remote signals or barrier semaphores. Data moves between devices by JAX's collectives and lax.ppermute only.
A program may use at most 64 MiB of HBM per device.

```python
import math
import jax
import jax.numpy as jnp
from jax import lax

D = 512
HID = 512
NC = 80
EDEV = 1024
TILE = 128
NODES = 20480
RB = 640
N_ROW = 32
N_COL = 8


def draw_edge_count(key, part):
    key = jax.random.fold_in(key, 5)
    first_key, second_key = jax.random.split(key)
    blocks = N_ROW * N_COL
    lowest = EDEV // (2 * TILE)
    counts = jax.random.randint(first_key, (blocks,), lowest, EDEV // TILE + 1) * TILE
    chosen = jax.random.randint(second_key, (), 0, blocks)
    counts = jnp.where(jnp.arange(blocks) == chosen, EDEV, counts)
    return counts.reshape(N_ROW, N_COL).astype(jnp.int32)


def draw_senders(key, part):
    key = jax.random.fold_in(key, 7)
    hot_key, other_key, perm_key, node_key = jax.random.split(key, 4)
    blocks = N_ROW * N_COL
    hot = jax.random.randint(hot_key, (N_COL,), 0, N_ROW)
    offset = jax.random.randint(other_key, (N_ROW, N_COL), 1, N_ROW)
    other = (hot[None, :] + offset) % N_ROW
    base = jnp.arange(EDEV, dtype=jnp.int32) % N_ROW
    owner = jnp.where(base[None, None, :] == other[:, :, None], hot[None, :, None], base[None, None, :])
    owner = owner.reshape(blocks, EDEV)
    keys = jax.random.split(perm_key, blocks)
    owner = jax.vmap(lambda k, o: jax.random.permutation(k, o))(keys, owner)
    local = jax.random.randint(node_key, (blocks, EDEV), 0, NC)
    return (owner * NC + local).reshape(N_ROW, N_COL, EDEV).astype(jnp.int32)


def set_ends(array, own_key, low, high):
    longest = array.shape.index(max(array.shape))
    spots = []
    for shift in (0, 1):
        where = [jax.random.randint(jax.random.fold_in(own_key, axis), (), 0, length) for axis, length in enumerate(array.shape)]
        where[longest] = (where[longest] + shift) % array.shape[longest]
        spots.append(tuple(where))
    return array.at[spots[0]].set(low).at[spots[1]].set(high)


def steps_of(rng, dims, pieces, smallest, top_value):
    gain = 1.0
    for dim, blocks in pieces:
        heights = jax.random.uniform(jax.random.fold_in(jax.random.fold_in(rng, 6), dim), (blocks,), jnp.float32, smallest / len(pieces), top_value / len(pieces))
        gain = gain * jnp.repeat(jnp.exp(heights), dims[dim] // blocks).reshape((-1,) + (1,) * (len(dims) - 1 - dim))
    return gain


def normal_values(stream_key, dims, deviation, bound, pieces=(), kind=jnp.bfloat16):
    values = deviation * jax.random.normal(stream_key, dims, jnp.float32)
    if pieces:
        values = values * steps_of(stream_key, dims, pieces, -0.22, 0.18)
    return jnp.clip(values, -bound, bound).astype(kind)


def setup_inputs(seed: int = 0) -> dict:
    seeds = jax.random.split(jax.random.key(seed), 12)
    node_latents = normal_values(seeds[0], (NODES, D), 1.0, 6.0, ((0, 256),))
    edge_latents = normal_values(seeds[1], (N_ROW, N_COL, EDEV, D), 1.0, 6.0, ((0, 32), (1, 8)))
    cotangent = normal_values(seeds[2], (N_ROW, N_COL, EDEV, D), 1.0, 6.0, ((0, 32), (1, 8)))
    senders = draw_senders(jax.random.fold_in(seeds[11], 71), 0)
    receivers = set_ends(jax.random.randint(seeds[4], (N_ROW, N_COL, EDEV), 0, RB), jax.random.fold_in(seeds[4], 1), 0, RB - 1).astype(jnp.int32)
    edge_count = draw_edge_count(jax.random.fold_in(seeds[11], 71), 0)
    w1 = normal_values(seeds[6], (3 * D, HID), (3 * D) ** -0.5, 0.15625)
    b1 = normal_values(seeds[7], (HID,), 1.0, 4.0, (), jnp.float32)
    w2 = normal_values(seeds[8], (HID, D), HID ** -0.5, 0.25)
    b2 = normal_values(seeds[9], (D,), 1.0, 4.0, (), jnp.float32)
    gamma = jnp.clip(jnp.exp(jax.random.uniform(seeds[10], (D,), jnp.float32, math.log(0.5), math.log(2.0))), 0.5, 2.0)
    return dict(node_latents=node_latents, edge_latents=edge_latents, cotangent=cotangent, senders=senders, receivers=receivers, edge_count=edge_count, w1=w1, b1=b1, w2=w2, b2=b2, gamma=gamma)


EPS = 1e-05

def contract_rows(left, right):
    return lax.dot_general(left, right, (((0,), (0,)), ((), ())), preferred_element_type=jnp.float32)

def edge_backward(inputs, cot_tile, w1, b1, w2, b2, gamma):
    pre_act = jnp.dot(inputs, w1, preferred_element_type=jnp.float32) + b1
    activ = jax.nn.silu(pre_act).astype(jnp.bfloat16)
    output = jnp.dot(activ, w2, preferred_element_type=jnp.float32) + b2
    centred = output - lax.optimization_barrier(jnp.mean(output, axis=1, keepdims=True))
    inv_std = lax.rsqrt(lax.optimization_barrier(jnp.mean(centred * centred, axis=1, keepdims=True)) + EPS)
    normed = centred * inv_std
    grad_z = cot_tile.astype(jnp.float32)
    grad_gain = lax.optimization_barrier(jnp.sum(grad_z * normed, axis=0))
    grad_norm = grad_z * gamma
    grad_out = inv_std * (grad_norm - lax.optimization_barrier(jnp.mean(grad_norm, axis=1, keepdims=True)) - normed * lax.optimization_barrier(jnp.mean(grad_norm * normed, axis=1, keepdims=True)))
    grad_outb = grad_out.astype(jnp.bfloat16)
    grad_bias2 = lax.optimization_barrier(jnp.sum(grad_out, axis=0))
    grad_mat2 = contract_rows(activ, grad_outb)
    grad_act = lax.dot_general(grad_outb, w2, (((1,), (1,)), ((), ())), preferred_element_type=jnp.float32)
    sigma = jax.nn.sigmoid(pre_act)
    grad_pre = grad_act * sigma * (1.0 + pre_act * (1.0 - sigma))
    grad_preb = grad_pre.astype(jnp.bfloat16)
    grad_bias1 = lax.optimization_barrier(jnp.sum(grad_pre, axis=0))
    return (grad_z, grad_preb, grad_mat2, grad_bias1, grad_bias2, grad_gain)

def reference(node_latents, edge_latents, cotangent, senders, receivers, edge_count, w1, b1, w2, b2, gamma):
    width = edge_latents.shape[3]
    slots = edge_latents.shape[2]
    hidden = w1.shape[1]
    send_size = NC * N_ROW

    def device_step(carry, flat):
        row_idx = (flat // N_COL).astype(jnp.int32)
        col_idx = (flat % N_COL).astype(jnp.int32)
        edges = edge_latents[row_idx, col_idx]
        cots = cotangent[row_idx, col_idx]
        send_global = (col_idx * send_size + senders[row_idx, col_idx]).astype(jnp.int32)
        recv_local = receivers[row_idx, col_idx]
        recv_global = ((recv_local // NC * N_ROW + row_idx) * NC + recv_local % NC).astype(jnp.int32)
        tile_count = (edge_count[row_idx, col_idx] // TILE).astype(jnp.int32)

        def tile_step(tile, inner):
            node_grad, acc_w1, acc_b1, acc_w2, acc_b2, acc_gain, grad_rows = inner
            start = (tile * TILE).astype(jnp.int32)
            edge_tile = lax.dynamic_slice_in_dim(edges, start, TILE, 0)
            cot_tile = lax.dynamic_slice_in_dim(cots, start, TILE, 0)
            send_ids = lax.dynamic_slice_in_dim(send_global, start, TILE, 0)
            recv_ids = lax.dynamic_slice_in_dim(recv_global, start, TILE, 0)
            inputs = jnp.concatenate([edge_tile, node_latents[send_ids], node_latents[recv_ids]], axis=1)
            grad_z, grad_preb, grad_mat2, grad_bias1, grad_bias2, grad_gain = edge_backward(inputs, cot_tile, w1, b1, w2, b2, gamma)
            grad_in = lax.dot_general(grad_preb, w1, (((1,), (1,)), ((), ())), preferred_element_type=jnp.float32)
            node_grad = node_grad.at[send_ids].add(grad_in[:, width:2 * width])
            node_grad = node_grad.at[recv_ids].add(grad_in[:, 2 * width:])
            new_rows = (grad_z + grad_in[:, :width]).astype(jnp.bfloat16)
            grad_rows = lax.dynamic_update_slice_in_dim(grad_rows, new_rows, start, 0)
            return (node_grad, acc_w1 + contract_rows(inputs, grad_preb), acc_b1 + grad_bias1, acc_w2 + grad_mat2, acc_b2 + grad_bias2, acc_gain + grad_gain, grad_rows)
        empty_rows = jnp.zeros((slots, width), jnp.bfloat16)
        result = lax.fori_loop(0, tile_count, tile_step, tuple(carry) + (empty_rows,))
        return (result[:6], result[6])
    init = (jnp.zeros((NC * N_ROW * N_COL, width), jnp.float32), jnp.zeros((3 * width, hidden), jnp.float32), jnp.zeros((hidden,), jnp.float32), jnp.zeros((hidden, width), jnp.float32), jnp.zeros((width,), jnp.float32), jnp.zeros((width,), jnp.float32))
    carry, rows = lax.scan(device_step, init, jnp.arange(N_ROW * N_COL, dtype=jnp.int32))
    node_grad, acc_w1, acc_b1, acc_w2, acc_b2, acc_gain = carry
    return (rows.reshape(N_ROW, N_COL, slots, width), node_grad, acc_w1, acc_b1, acc_w2, acc_b2, acc_gain)
```

```python
import functools

import jax
import jax.numpy as jnp
from jax import lax
from jax.experimental import pallas as pl
from jax.experimental.pallas import tpu as pltpu
from jax.sharding import Mesh, PartitionSpec as P

EPS = 1e-05
NX, NZ, NY, NCORE = 4, 8, 4, 2
BF16 = jnp.bfloat16
F32 = jnp.float32


def shift(value, axis, size, step):
    return lax.ppermute(value, axis, [(i, (i - step) % size) for i in range(size)])


def push(value, axis, size, step):
    return lax.ppermute(value, axis, [(i, (i + step) % size) for i in range(size)])


def gather_send(own):
    half = own.shape[1] // 2
    own_a, own_b = own[:, :half], own[:, half:]
    along_x = jnp.stack([own_a] + [shift(own_a, "x", NX, d) for d in (1, 2, 3)])
    a = {0: along_x}
    for d in (1, 2, 3):
        a[d] = shift(a[d - 1], "z", NZ, 1)
        a[NZ - d] = shift(a[(NZ - d + 1) % NZ], "z", NZ, -1)
    a4_lo = shift(a[3][:2], "z", NZ, 1)
    a4_hi = shift(a[5][2:], "z", NZ, -1)
    along_z = jnp.stack([own_b] + [shift(own_b, "z", NZ, d) for d in range(1, NZ)])
    b1 = shift(along_z, "x", NX, 1)
    b3 = shift(along_z, "x", NX, -1)
    b2_lo = shift(b1[:4], "x", NX, 1)
    b2_hi = shift(b3[4:], "x", NX, -1)
    pieces_a = [a[0], a[1], a[2], a[3], a4_lo, a4_hi, a[5], a[6], a[7]]
    pieces_b = [along_z, b1, b2_lo, b2_hi, b3]
    return pieces_a, pieces_b


def gather_recv(own):
    along_y = jnp.stack([own] + [shift(own, "y", NY, d) for d in (1, 2, 3)])
    return along_y, shift(along_y, "core", NCORE, 1)


def place_a():
    return [(0, 0, 4), (1, 0, 4), (2, 0, 4), (3, 0, 4), (4, 0, 2), (4, 2, 2), (5, 0, 4), (6, 0, 4), (7, 0, 4)]


def place_b():
    return [(0, 0, 8), (1, 0, 8), (2, 0, 4), (2, 4, 4), (3, 0, 8)]


def mm(a, b, dims):
    return lax.dot_general(a, b, ((dims[0], dims[1]), ((), ())), preferred_element_type=F32)


def edge_kernel_body(tile, scalars, *refs):
    (sid_col, rid_col, sid_row, rid_row, edges, cots, w1, w2, b1, b2, gamma) = refs[:11]
    pieces_a, pieces_b, pieces_r = refs[11:20], refs[20:25], refs[25:27]
    out = refs[27:]
    grad_edges, s_a, s_b, s_r = out[0], out[1:10], out[10:15], out[15:17]
    w_own, w_peer, small = out[17:20]
    lat_a, lat_b, lat_r, x_s, x_r, preb, activ, goutb, sems = out[20:]
    count, core = scalars[0], scalars[1]
    slots, width = edges.shape
    half = width // 2
    nodes = lat_a.shape[0] * lat_a.shape[1] * lat_a.shape[2]
    block = lat_r.shape[0] * lat_r.shape[1]

    copies = []
    for ref, (dz, dx, n) in zip(pieces_a, place_a()):
        copies.append((ref, lat_a.at[dz, pl.ds(dx, n)]))
    for ref, (dx, dz, n) in zip(pieces_b, place_b()):
        copies.append((ref, lat_b.at[pl.ds(dz, n), dx]))
    for core_at, ref in enumerate(pieces_r):
        copies.append((ref, lat_r.at[pl.ds(core_at * NY, NY)]))
    copies = [pltpu.make_async_copy(src, dst, sems.at[i]) for i, (src, dst) in enumerate(copies)]
    for copy in copies:
        copy.start()
    for copy in copies:
        copy.wait()

    mat_a = lat_a[...].reshape(nodes, half)
    mat_b = lat_b[...].reshape(nodes, half)
    mat_r = lat_r[...].reshape(block, width)

    def one_hot(hit):
        return jnp.where(hit, 1.0, 0.0).astype(BF16)

    def step(t, sums):
        sum_b1, sum_b2, sum_gain = sums
        rows = pl.ds(pl.multiple_of(t * tile, tile), tile)
        hot_s = one_hot(sid_col[rows, :] == lax.broadcasted_iota(jnp.int32, (tile, nodes), 1))
        hot_r = one_hot(rid_col[rows, :] == lax.broadcasted_iota(jnp.int32, (tile, block), 1))
        xs = jnp.concatenate([mm(hot_s, mat_a, ((1,), (0,))), mm(hot_s, mat_b, ((1,), (0,)))], axis=1).astype(BF16)
        xr = mm(hot_r, mat_r, ((1,), (0,))).astype(BF16)
        x_s[rows, :] = xs
        x_r[rows, :] = xr
        pre = (
            mm(edges[rows, :], w1[0:width, :], ((1,), (0,)))
            + mm(xs, w1[width : 2 * width, :], ((1,), (0,)))
            + mm(xr, w1[2 * width :, :], ((1,), (0,)))
            + b1[...]
        )
        sigma = jax.nn.sigmoid(pre)
        act = (pre * sigma).astype(BF16)
        slope = sigma * (1.0 + pre * (1.0 - sigma))
        activ[rows, :] = act
        output = mm(act, w2[...], ((1,), (0,))) + b2[...]
        centred = output - jnp.mean(output, axis=1, keepdims=True)
        inv_std = lax.rsqrt(jnp.mean(centred * centred, axis=1, keepdims=True) + EPS)
        normed = centred * inv_std
        live = t * tile + lax.broadcasted_iota(jnp.int32, (tile, 1), 0) < count
        g = jnp.where(live, cots[rows, :].astype(F32), 0.0)
        sum_gain = sum_gain + jnp.sum(g * normed, axis=0, keepdims=True)
        grad_norm = g * gamma[...]
        grad_out = inv_std * (
            grad_norm
            - jnp.mean(grad_norm, axis=1, keepdims=True)
            - normed * jnp.mean(grad_norm * normed, axis=1, keepdims=True)
        )
        gob = grad_out.astype(BF16)
        goutb[rows, :] = gob
        sum_b2 = sum_b2 + jnp.sum(grad_out, axis=0, keepdims=True)
        grad_pre = mm(gob, w2[...], ((1,), (1,))) * slope
        sum_b1 = sum_b1 + jnp.sum(grad_pre, axis=0, keepdims=True)
        gpb = grad_pre.astype(BF16)
        preb[rows, :] = gpb
        grad_edges[rows, :] = (g + mm(gpb, w1[0:width, :], ((1,), (1,)))).astype(BF16)
        return sum_b1, sum_b2, sum_gain

    zero = jnp.zeros((1, width), F32)
    sum_b1, sum_b2, sum_gain = lax.fori_loop(0, slots // tile, step, (zero, zero, zero))
    small[...] = jnp.concatenate([sum_b1, sum_b2, sum_gain, jnp.zeros((5, width), F32)], axis=0)

    grads = preb[...]

    def node_rows(ids, first, n):
        hit = ids[...] == first + lax.broadcasted_iota(jnp.int32, (n, slots), 0)
        return mm(one_hot(hit), grads, ((1,), (0,))).astype(BF16)

    share = lat_a.shape[2]
    at_a = {(dz, dx + i): (ref, i) for ref, (dz, dx, n) in zip(s_a, place_a()) for i in range(n)}
    at_b = {(dz + i, dx): (ref, i) for ref, (dx, dz, n) in zip(s_b, place_b()) for i in range(n)}
    for dz in range(NZ):
        sums = node_rows(sid_row, dz * NX * share, NX * share)
        for dx in range(NX):
            part = sums[dx * share : (dx + 1) * share, :]
            ref, i = at_a[dz, dx]
            ref[i] = part[:, :half]
            ref, i = at_b[dz, dx]
            ref[i] = part[:, half:]
    for core_at in range(NCORE):
        s_r[core_at][...] = node_rows(rid_row, core_at * NY * share, NY * share).reshape(NY, share, width)

    own = pl.ds(pl.multiple_of(core * half, half), half)
    peer = pl.ds(pl.multiple_of((1 - core) * half, half), half)
    for cols, ref in ((peer, w_peer), (own, w_own)):
        for i, left in enumerate((edges, x_s, x_r)):
            ref[i * width : (i + 1) * width, :] = mm(left[...], preb[:, cols], ((0,), (0,))).astype(ref.dtype)
        ref[3 * width :, :] = mm(activ[...], goutb[:, cols], ((0,), (0,))).astype(ref.dtype)


def edge_kernel(scalars, sid, rid, edges, cots, w1, w2, b1, b2, gamma, pieces_a, pieces_b, pieces_r):
    slots, width = edges.shape
    half = width // 2
    share = pieces_a[0].shape[1]
    tile = 256
    vmem = pl.BlockSpec(memory_space=pltpu.VMEM)
    hbm = pl.BlockSpec(memory_space=pl.ANY)
    shaped = jax.ShapeDtypeStruct
    out_shape = (
        [shaped((slots, width), BF16)]
        + [shaped(p.shape, BF16) for p in pieces_a]
        + [shaped(p.shape, BF16) for p in pieces_b]
        + [shaped(p.shape, BF16) for p in pieces_r]
        + [shaped((4 * width, half), F32), shaped((4 * width, half), BF16), shaped((8, width), F32)]
    )
    outs = pl.pallas_call(
        functools.partial(edge_kernel_body, tile),
        out_shape=out_shape,
        in_specs=[pl.BlockSpec(memory_space=pltpu.SMEM)] + [vmem] * 11 + [hbm] * 16,
        out_specs=[vmem] * 20,
        scratch_shapes=[
            pltpu.VMEM((NZ, NX, share, half), BF16),
            pltpu.VMEM((NZ, NX, share, half), BF16),
            pltpu.VMEM((NCORE * NY, share, width), BF16),
            pltpu.VMEM((slots, width), BF16),
            pltpu.VMEM((slots, width), BF16),
            pltpu.VMEM((slots, width), BF16),
            pltpu.VMEM((slots, width), BF16),
            pltpu.VMEM((slots, width), BF16),
            pltpu.SemaphoreType.DMA((16,)),
        ],
        compiler_params=pltpu.CompilerParams(vmem_limit_bytes=56 * 2**20),
        cost_estimate=pl.CostEstimate(flops=13_000_000_000, bytes_accessed=16_000_000, transcendentals=1_000_000),
        name="edge_step",
    )(
        scalars,
        sid.reshape(slots, 1),
        rid.reshape(slots, 1),
        sid.reshape(1, slots),
        rid.reshape(1, slots),
        edges,
        cots,
        w1,
        w2,
        b1.reshape(1, width),
        b2.reshape(1, width),
        gamma.reshape(1, width),
        *pieces_a,
        *pieces_b,
        *pieces_r,
    )
    return outs[0], outs[1:10], outs[10:15], outs[15:17], outs[17], outs[18], outs[19]


def add(mine, *others):
    total = mine.astype(F32)
    for other in others:
        total = total + other.astype(F32)
    return total


def reduce_send(s_a, s_b):
    a0, a1, a2, a3, a4_lo, a4_hi, a5, a6, a7 = s_a
    up = push(a4_lo, "z", NZ, 1)
    down = push(a4_hi, "z", NZ, -1)
    up = jnp.concatenate([add(a3[:2], up).astype(BF16), a3[2:]])
    down = jnp.concatenate([a5[:2], add(a5[2:], down).astype(BF16)])
    for mine_up, mine_down in ((a2, a6), (a1, a7)):
        up = add(mine_up, push(up, "z", NZ, 1)).astype(BF16)
        down = add(mine_down, push(down, "z", NZ, -1)).astype(BF16)
    total = add(a0, push(up, "z", NZ, 1), push(down, "z", NZ, -1))
    rounded = total.astype(BF16)
    total_a = add(total[0], *[push(rounded[d], "x", NX, d) for d in (1, 2, 3)])
    b0, b1, b2_lo, b2_hi, b3 = s_b
    up = push(b2_lo, "x", NX, 1)
    down = push(b2_hi, "x", NX, -1)
    up = jnp.concatenate([add(b1[:4], up).astype(BF16), b1[4:]])
    down = jnp.concatenate([b3[:4], add(b3[4:], down).astype(BF16)])
    total = add(b0, push(up, "x", NX, 1), push(down, "x", NX, -1))
    rounded = total.astype(BF16)
    total_b = add(total[0], *[push(rounded[d], "z", NZ, d) for d in range(1, NZ)])
    return total_a, total_b


def reduce_recv(s_r):
    total = add(s_r[0], push(s_r[1], "core", NCORE, 1))
    rounded = total.astype(BF16)
    return add(total[0], *[push(rounded[d], "y", NY, d) for d in (1, 2, 3)])


def split_small(small):
    values = small[:3].reshape(6, -1)
    high = values.astype(BF16)
    low = (values - high.astype(F32)).astype(BF16)
    return jnp.concatenate([high, low, jnp.zeros((4, values.shape[1]), BF16)])


def join_small(rows):
    rows = rows.astype(F32)
    return rows[:6] + rows[6:12]


def reduce_axis(value, small, axis, size):
    rows = value.shape[0] // size
    me = lax.axis_index(axis)
    parts = value.reshape(size, rows, value.shape[1])
    packed = split_small(small)
    total = lax.dynamic_index_in_dim(parts, me, 0, False).astype(F32)
    smalls = jnp.zeros((size,) + packed.shape, BF16)
    smalls = lax.dynamic_update_index_in_dim(smalls, packed, me, 0)
    for d in range(1, size):
        part = lax.dynamic_index_in_dim(parts, (me + d) % size, 0, False).astype(BF16)
        got = push(jnp.concatenate([part, packed]), axis, size, d)
        total = total + got[:rows].astype(F32)
        smalls = lax.dynamic_update_index_in_dim(smalls, got[rows:], (me - d) % size, 0)
    return total, add_smalls(smalls)


def add_smalls(smalls):
    total = join_small(smalls[0])
    for i in range(1, smalls.shape[0]):
        total = total + join_small(smalls[i])
    return total.reshape(3, -1)


def gather_axis(value, axis, size):
    me = lax.axis_index(axis)
    out = jnp.zeros((size,) + value.shape, value.dtype)
    out = lax.dynamic_update_index_in_dim(out, value, me, 0)
    for d in range(1, size):
        out = lax.dynamic_update_index_in_dim(out, shift(value, axis, size, d), (me + d) % size, 0)
    return out.reshape((-1,) + value.shape[1:])


def reduce_weights(w_own, w_peer, small):
    packed = split_small(small)
    got = push(jnp.concatenate([w_peer, packed]), "core", NCORE, 1)
    rows = w_peer.shape[0]
    total = w_own + got[:rows].astype(F32)
    small_total = (join_small(packed) + join_small(got[rows:])).reshape(3, -1)
    for axis, size in (("y", NY), ("x", NX), ("z", NZ)):
        total, small_total = reduce_axis(total, small_total, axis, size)
    value = total.astype(BF16)
    for axis, size in (("z", NZ), ("x", NX), ("y", NY)):
        value = gather_axis(value, axis, size)
    other = push(value, "core", NCORE, 1)
    first = lax.axis_index("core") == 0
    left = jnp.where(first, value, other)
    right = jnp.where(first, other, value)
    weights = jnp.concatenate([left, right], axis=1).astype(F32)
    return weights, small_total


def local(node_latents, edge_latents, cotangent, senders, receivers, edge_count, w1, b1, w2, b2, gamma):
    slots, width = edge_latents.shape[2:]
    share = node_latents.shape[0]
    edges = edge_latents.reshape(slots, width)
    cots = cotangent.reshape(slots, width)
    x, z, y, core = [lax.axis_index(name) for name in ("x", "z", "y", "core")]

    pieces_a, pieces_b = gather_send(node_latents)
    pieces_r = gather_recv(node_latents)

    send = senders.reshape(slots)
    owner, rest = send // share, send % share
    sid = (((owner % NZ - z) % NZ) * NX + (owner // NZ - x) % NX) * share + rest
    recv = receivers.reshape(slots)
    owner, rest = recv // share, recv % share
    rid = (((owner % NCORE - core) % NCORE) * NY + (owner // NCORE - y) % NY) * share + rest
    scalars = jnp.stack([edge_count.reshape(()), core.astype(jnp.int32)])

    grad_edges, s_a, s_b, s_r, w_own, w_peer, small = edge_kernel(
        scalars, sid, rid, edges, cots, w1, w2, b1, b2, gamma, pieces_a, pieces_b, pieces_r
    )
    weights, small_total = reduce_weights(w_own, w_peer, small)
    total_a, total_b = reduce_send(s_a, s_b)
    total_r = reduce_recv(s_r)
    sums = jnp.concatenate([total_a, total_b, total_r], axis=1).astype(BF16)
    half = width // 2
    grad_nodes = mm(sums[:, :width], w1[width : 2 * width], ((1,), (1,))) + mm(
        sums[:, width:], w1[2 * width :], ((1,), (1,))
    )
    return (
        grad_edges.reshape(1, 1, slots, width),
        grad_nodes,
        weights[: 3 * width],
        small_total[0],
        weights[3 * width :],
        small_total[1],
        small_total[2],
    )


def solution(mesh):
    mesh = Mesh(mesh.devices.reshape(NX, NZ, NY, NCORE), ("x", "z", "y", "core"))
    row, col = ("x", "z"), ("y", "core")
    in_specs = (
        P(col + row, None),
        P(row, col, None, None),
        P(row, col, None, None),
        P(row, col, None),
        P(row, col, None),
        P(row, col),
        P(),
        P(),
        P(),
        P(),
        P(),
    )
    out_specs = (P(row, col, None, None), P(col + row, None), P(), P(), P(), P(), P())
    return jax.shard_map(local, mesh=mesh, in_specs=in_specs, out_specs=out_specs, check_vma=False)
```

```python
import functools

import jax
import jax.numpy as jnp
from jax import lax
from jax.experimental import pallas as pl
from jax.experimental.pallas import tpu as pltpu
from jax.sharding import Mesh, PartitionSpec as P

EPS = 1e-05
NX, NZ, NY, NCORE = 4, 8, 4, 2
BF16 = jnp.bfloat16
F32 = jnp.float32


def shift(value, axis, size, step):
    return lax.ppermute(value, axis, [(i, (i - step) % size) for i in range(size)])


def push(value, axis, size, step):
    return lax.ppermute(value, axis, [(i, (i + step) % size) for i in range(size)])


def gather_send(own):
    along_x = jnp.stack([own] + [shift(own, "x", NX, d) for d in (1, 2, 3)])
    a = {0: along_x}
    for d in (1, 2, 3):
        a[d] = shift(a[d - 1], "z", NZ, 1)
        a[NZ - d] = shift(a[(NZ - d + 1) % NZ], "z", NZ, -1)
    a4_lo = shift(a[3][:2], "z", NZ, 1)
    a4_hi = shift(a[5][2:], "z", NZ, -1)
    return [a[0], a[1], a[2], a[3], a4_lo, a4_hi, a[5], a[6], a[7]]


def gather_recv(own):
    along_y = jnp.stack([own] + [shift(own, "y", NY, d) for d in (1, 2, 3)])
    return along_y, shift(along_y, "core", NCORE, 1)


PLACES = [(0, 0, 4), (1, 0, 4), (2, 0, 4), (3, 0, 4), (4, 0, 2), (4, 2, 2), (5, 0, 4), (6, 0, 4), (7, 0, 4)]
SMALL = 16


def mm(a, b, dims):
    return lax.dot_general(a, b, ((dims[0], dims[1]), ((), ())), preferred_element_type=F32)


def one_hot(hit):
    return jnp.where(hit, 1.0, 0.0).astype(BF16)


def split_rows(values):
    high = values.astype(BF16).astype(F32)
    return jnp.concatenate([high, values - high, jnp.zeros((4, values.shape[1]), F32)], axis=0).astype(BF16)


def join_rows(rows):
    rows = rows.astype(F32)
    return rows[0:6] + rows[6:12]


def call(body, out_shape, args, name, scalars=(), scratch=(), flops=1_000_000, where=None, limit=24):
    vmem = pl.BlockSpec(memory_space=pltpu.VMEM)
    bytes_accessed = sum(a.size * a.dtype.itemsize for a in list(args) + list(out_shape))
    return pl.pallas_call(
        body,
        out_shape=out_shape,
        in_specs=[pl.BlockSpec(memory_space=pltpu.SMEM)] * len(scalars) + (where or [vmem] * len(args)),
        out_specs=[vmem] * len(out_shape),
        scratch_shapes=list(scratch),
        compiler_params=pltpu.CompilerParams(vmem_limit_bytes=limit * 2**20),
        cost_estimate=pl.CostEstimate(flops=flops, bytes_accessed=bytes_accessed, transcendentals=0),
        name=name,
    )(*scalars, *args)


def shaped(*shape, dtype=BF16):
    return jax.ShapeDtypeStruct(shape, dtype)


def edge_kernel_body(tile, scalars, *refs):
    sid_col, rid_col, rid_row, b1, b2, gamma = refs[:6]
    edges_hbm, cots_hbm, w1_hbm, w2_hbm = refs[6:10]
    pieces_s, pieces_r = refs[10:19], refs[19:21]
    grad_edges, preb_out, pay, own_w, own_r, own_small = refs[21:27]
    lat_s, lat_r, lefts, cots, w1, w2, rights, sems = refs[27:]
    count, core, y = scalars[0], scalars[1], scalars[2]
    slots, width = cots.shape
    half = width // 2
    share = lat_s.shape[2]
    nodes = NZ * NX * share
    block = NCORE * NY * share
    edges, x_s, x_r, activ = [lefts.at[i] for i in range(4)]
    preb, goutb = rights.at[0], rights.at[1]

    copies = [(ref, lat_s.at[dz, pl.ds(dx, n)]) for ref, (dz, dx, n) in zip(pieces_s, PLACES)]
    copies += [(ref, lat_r.at[pl.ds(i * NY, NY)]) for i, ref in enumerate(pieces_r)]
    copies += [(edges_hbm, edges), (w1_hbm, w1), (w2_hbm, w2), (cots_hbm, cots)]
    copies = [pltpu.make_async_copy(src, dst, sems.at[i]) for i, (src, dst) in enumerate(copies)]
    for copy in copies:
        copy.start()
    for copy in copies:
        copy.wait()

    mat_s = lat_s[...].reshape(nodes, width)
    mat_r = lat_r[...].reshape(block, width)

    def step(t, sums):
        sum_b1, sum_b2, sum_gain = sums
        rows = pl.ds(pl.multiple_of(t * tile, tile), tile)
        hot_s = one_hot(sid_col[rows, :] == lax.broadcasted_iota(jnp.int32, (tile, nodes), 1))
        hot_r = one_hot(rid_col[rows, :] == lax.broadcasted_iota(jnp.int32, (tile, block), 1))
        xs = mm(hot_s, mat_s, ((1,), (0,))).astype(BF16)
        xr = mm(hot_r, mat_r, ((1,), (0,))).astype(BF16)
        x_s[rows, :] = xs
        x_r[rows, :] = xr
        pre = (
            mm(edges[rows, :], w1[0:width, :], ((1,), (0,)))
            + mm(xs, w1[width : 2 * width, :], ((1,), (0,)))
            + mm(xr, w1[2 * width :, :], ((1,), (0,)))
            + b1[...]
        )
        sigma = jax.nn.sigmoid(pre)
        act = (pre * sigma).astype(BF16)
        slope = sigma * (1.0 + pre * (1.0 - sigma))
        activ[rows, :] = act
        output = mm(act, w2[...], ((1,), (0,))) + b2[...]
        centred = output - jnp.mean(output, axis=1, keepdims=True)
        inv_std = lax.rsqrt(jnp.mean(centred * centred, axis=1, keepdims=True) + EPS)
        normed = centred * inv_std
        live = t * tile + lax.broadcasted_iota(jnp.int32, (tile, 1), 0) < count
        g = jnp.where(live, cots[rows, :].astype(F32), 0.0)
        sum_gain = sum_gain + jnp.sum(g * normed, axis=0, keepdims=True)
        grad_norm = g * gamma[...]
        grad_out = inv_std * (
            grad_norm
            - jnp.mean(grad_norm, axis=1, keepdims=True)
            - normed * jnp.mean(grad_norm * normed, axis=1, keepdims=True)
        )
        gob = grad_out.astype(BF16)
        goutb[rows, :] = gob
        sum_b2 = sum_b2 + jnp.sum(grad_out, axis=0, keepdims=True)
        grad_pre = mm(gob, w2[...], ((1,), (1,))) * slope
        sum_b1 = sum_b1 + jnp.sum(grad_pre, axis=0, keepdims=True)
        gpb = grad_pre.astype(BF16)
        preb[rows, :] = gpb
        grad_edges[rows, :] = (g + mm(gpb, w1[0:width, :], ((1,), (1,)))).astype(BF16)
        return sum_b1, sum_b2, sum_gain

    zero = jnp.zeros((1, width), F32)
    sums = lax.fori_loop(0, slots // tile, step, (zero, zero, zero))
    preb_out[...] = preb[...]

    own = pl.ds(pl.multiple_of(core * half, half), half)
    peer = pl.ds(pl.multiple_of((1 - core) * half, half), half)
    for d in range(NY):
        i = lax.rem(y + d, NY)
        right = jnp.where(i == NY - 1, 1, 0)
        rows = slice(d * width, (d + 1) * width)
        pay[rows, :] = mm(lefts[i], rights[right, :, peer], ((0,), (0,))).astype(BF16)
        own_w[rows, :] = mm(lefts[i], rights[right, :, own], ((0,), (0,)))

    first = NY * width
    for core_at in range(NCORE):
        ids = core_at * NY * share + lax.broadcasted_iota(jnp.int32, (NY * share, slots), 0)
        sums_r = mm(one_hot(rid_row[...] == ids), preb[...], ((1,), (0,)))
        for d in range(NY):
            for h in range(2):
                part = sums_r[d * share : (d + 1) * share, h * half : (h + 1) * half]
                at = (2 * d + h) * share
                if core_at == 0:
                    own_r[at : at + share, :] = part
                else:
                    pay[first + at : first + at + share, :] = part.astype(BF16)
    parts = [s[:, h * half : (h + 1) * half] for s in sums for h in range(2)]
    small = split_rows(jnp.concatenate(parts, axis=0))
    own_small[...] = small
    at = first + 2 * NY * share
    pay[at : at + SMALL, :] = small


def edge_kernel(scalars, sid, rid, edges, cots, w1, w2, b1, b2, gamma, pieces_s, pieces_r):
    slots, width = edges.shape
    half = width // 2
    share = pieces_s[0].shape[1]
    vmem = pl.BlockSpec(memory_space=pltpu.VMEM)
    hbm = pl.BlockSpec(memory_space=pl.ANY)
    recv_rows = 2 * NY * share
    return call(
        functools.partial(edge_kernel_body, 256),
        [
            shaped(slots, width),
            shaped(slots, width),
            shaped(NY * width + recv_rows + SMALL, half),
            shaped(NY * width, half, dtype=F32),
            shaped(recv_rows, half, dtype=F32),
            shaped(SMALL, half),
        ],
        [
            sid.reshape(slots, 1),
            rid.reshape(slots, 1),
            rid.reshape(1, slots),
            b1.reshape(1, width),
            b2.reshape(1, width),
            gamma.reshape(1, width),
            edges,
            cots,
            w1,
            w2,
            *pieces_s,
            *pieces_r,
        ],
        "edge_step",
        scalars=[scalars],
        where=[vmem] * 6 + [hbm] * 15,
        scratch=[
            pltpu.VMEM((NZ, NX, share, width), BF16),
            pltpu.VMEM((NCORE * NY, share, width), BF16),
            pltpu.VMEM((4, slots, width), BF16),
            pltpu.VMEM((slots, width), BF16),
            pltpu.VMEM(w1.shape, BF16),
            pltpu.VMEM(w2.shape, BF16),
            pltpu.VMEM((2, slots, width), BF16),
            pltpu.SemaphoreType.DMA((15,)),
        ],
        flops=10_000_000_000,
        limit=56,
    )


def scatter_body(sid_row, preb, *outs):
    slots, width = preb.shape
    share = outs[0].shape[1]
    grads = preb[...]
    for ref, (dz, dx, n) in zip(outs, PLACES):
        first = (dz * NX + dx) * share
        hit = sid_row[...] == first + lax.broadcasted_iota(jnp.int32, (n * share, slots), 0)
        ref[...] = mm(one_hot(hit), grads, ((1,), (0,))).astype(BF16).reshape(n, share, width)


def scatter_kernel(sid, preb, share):
    slots, width = preb.shape
    out_shape = [shaped(n, share, width) for _, _, n in PLACES]
    return call(scatter_body, out_shape, [sid.reshape(1, slots), preb], "scatter", flops=3_000_000_000, limit=48)


def add_body(first, mine, got, out):
    n = got.shape[0]
    out[...] = mine[...]
    out[first : first + n] = (mine[first : first + n].astype(F32) + got[...].astype(F32)).astype(BF16)


def add_piece(mine, got, first=0):
    return call(functools.partial(add_body, first), [shaped(*mine.shape)], [mine, got], "add_piece")[0]


def turn_body(mine, up, down, keep, *sends):
    total = mine[...].astype(F32) + up[...].astype(F32) + down[...].astype(F32)
    keep[...] = total[0]
    for d, ref in enumerate(sends):
        ref[...] = total[d + 1].astype(BF16)


def reduce_send(pieces):
    a0, a1, a2, a3, a4_lo, a4_hi, a5, a6, a7 = pieces
    share, width = a0.shape[1:]
    up = add_piece(a3, push(a4_lo, "z", NZ, 1), 0)
    down = add_piece(a5, push(a4_hi, "z", NZ, -1), 2)
    for mine_up, mine_down in ((a2, a6), (a1, a7)):
        up = add_piece(mine_up, push(up, "z", NZ, 1))
        down = add_piece(mine_down, push(down, "z", NZ, -1))
    up, down = push(up, "z", NZ, 1), push(down, "z", NZ, -1)
    out_shape = [shaped(share, width, dtype=F32)] + [shaped(share, width)] * 3
    keep, *sends = call(turn_body, out_shape, [a0, up, down], "turn")
    return [keep] + [push(part, "x", NX, d + 1) for d, part in enumerate(sends)]


def core_body(own_w, own_r, own_small, got, keep, small, *sends):
    rows, recv = own_w.shape[0] // NY, own_r.shape[0] // NY
    first = own_w.shape[0]
    at = first + own_r.shape[0]
    summed = split_rows(join_rows(own_small[...]) + join_rows(got[at : at + SMALL, :]))
    small[...] = summed
    for d in range(NY):
        total_w = own_w[d * rows : (d + 1) * rows, :] + got[d * rows : (d + 1) * rows, :].astype(F32)
        total_r = own_r[d * recv : (d + 1) * recv, :] + got[first + d * recv : first + (d + 1) * recv, :].astype(F32)
        if d == 0:
            keep[0:rows, :] = total_w
            keep[rows : rows + recv, :] = total_r
        else:
            ref = sends[d - 1]
            ref[0:rows, :] = total_w.astype(BF16)
            ref[rows : rows + recv, :] = total_r.astype(BF16)
            ref[rows + recv : rows + recv + SMALL, :] = summed


def add_smalls(smalls, own, gots, me, size):
    smalls[me] = own
    for d, got in enumerate(gots):
        smalls[lax.rem(me + size - 1 - d, size)] = got
    total = join_rows(smalls[0])
    for i in range(1, size):
        total = total + join_rows(smalls[i])
    return split_rows(total)


def along_y_body(place, keep, small, got1, got2, got3, recv, keep_x, small_x, send1, send2, send3, total, smalls):
    x, y = place[0], place[1]
    rows = total.shape[0]
    gots = (got1, got2, got3)
    n = keep.shape[0]
    summed = keep[...]
    for got in gots:
        summed = summed + got[0:n, :].astype(F32)
    total[...] = summed[0:rows, :]
    recv[...] = summed[rows:, :]
    small_x[...] = add_smalls(smalls, small[...], [got[n : n + SMALL, :] for got in gots], y, NY)
    part = rows // NX
    keep_x[...] = total[pl.ds(pl.multiple_of(x * part, part), part), :]
    for d, ref in ((1, send1), (2, send2), (3, send3)):
        at = pl.multiple_of(lax.rem(x + d, NX) * part, part)
        ref[0:part, :] = total[pl.ds(at, part), :].astype(BF16)
        ref[part : part + SMALL, :] = small_x[...]


def along_x_body(place, keep, small, got1, got2, got3, out, smalls):
    gots = (got1, got2, got3)
    n = keep.shape[0]
    summed = keep[...]
    for got in gots:
        summed = summed + got[0:n, :].astype(F32)
    out[0:n, :] = summed.astype(BF16)
    out[n : n + SMALL, :] = add_smalls(smalls, small[...], [got[n : n + SMALL, :] for got in gots], place[0], NX)


def merge_body(a, b, out):
    n = a.shape[0] - SMALL
    out[0:n, :] = (a[0:n, :].astype(F32) + b[0:n, :].astype(F32)).astype(BF16)
    out[n : n + SMALL, :] = split_rows(join_rows(a[n : n + SMALL, :]) + join_rows(b[n : n + SMALL, :]))


def last_merge_body(a, b, out, small):
    n = a.shape[0] - SMALL
    out[...] = (a[0:n, :].astype(F32) + b[0:n, :].astype(F32)).astype(BF16)
    small[...] = join_rows(a[n : n + SMALL, :]) + join_rows(b[n : n + SMALL, :])


def lay_x_body(place, own, got1, got2, got3, out):
    n = own.shape[0]
    for d, ref in enumerate((own, got1, got2, got3)):
        at = pl.multiple_of(lax.rem(place[0] + d, NX) * n, n)
        out[pl.ds(at, n), :] = ref[...]


def lay_weights_body(place, *refs):
    mine, other, grad_w1, grad_w2 = refs[:NY], refs[NY : 2 * NY], refs[-2], refs[-1]
    n, half = mine[0].shape
    first = place[2] == 0
    for d in range(NY):
        i = lax.rem(place[1] + d, NY)
        a, b = mine[d][...].astype(F32), other[d][...].astype(F32)
        left, right = jnp.where(first, a, b), jnp.where(first, b, a)

        @pl.when(i < NY - 1)
        def _():
            rows = pl.ds(pl.multiple_of(i * n, n), n)
            grad_w1[rows, 0:half] = left
            grad_w1[rows, half : 2 * half] = right

        @pl.when(i == NY - 1)
        def _():
            grad_w2[:, 0:half] = left
            grad_w2[:, half : 2 * half] = right


def reduce_weights(place, pay, own_w, own_r, own_small):
    half = pay.shape[1]
    rows, recv = own_w.shape[0] // NY, own_r.shape[0] // NY
    got = push(pay, "core", NCORE, 1)
    out_shape = [shaped(rows + recv, half, dtype=F32), shaped(SMALL, half)] + [shaped(rows + recv + SMALL, half)] * 3
    keep, small, *sends = call(core_body, out_shape, [own_w, own_r, own_small, got], "after_core")
    gots = [push(part, "y", NY, d + 1) for d, part in enumerate(sends)]
    part = rows // NX
    recv_sum, keep, small, *sends = call(
        along_y_body,
        [shaped(recv, half, dtype=F32), shaped(part, half, dtype=F32), shaped(SMALL, half)]
        + [shaped(part + SMALL, half)] * 3,
        [keep, small, *gots],
        "after_y",
        scalars=[place],
        scratch=[pltpu.VMEM((rows, half), F32), pltpu.VMEM((NY, SMALL, half), BF16)],
    )
    gots = [push(part, "x", NX, d + 1) for d, part in enumerate(sends)]
    value = call(
        along_x_body,
        [shaped(part + SMALL, half)],
        [keep, small, *gots],
        "after_x",
        scalars=[place],
        scratch=[pltpu.VMEM((NX, SMALL, half), BF16)],
    )[0]
    for bit in (1, 2, 4):
        got = lax.ppermute(value, "z", [(i, i ^ bit) for i in range(NZ)])
        if bit < 4:
            value = call(merge_body, [shaped(*value.shape)], [value, got], "merge")[0]
    value, small = call(
        last_merge_body, [shaped(part, half), shaped(6, half, dtype=F32)], [value, got], "last_merge"
    )
    gots = [shift(value, "x", NX, d) for d in (1, 2, 3)]
    value = call(lay_x_body, [shaped(rows, half)], [value, *gots], "lay_x", scalars=[place])[0]
    mine = [value] + [shift(value, "y", NY, d) for d in (1, 2, 3)]
    other = [push(part, "core", NCORE, 1) for part in mine]
    grad_w1, grad_w2 = call(
        lay_weights_body,
        [shaped(3 * rows, 2 * half, dtype=F32), shaped(rows, 2 * half, dtype=F32)],
        mine + other,
        "lay_weights",
        scalars=[place],
    )
    return grad_w1, grad_w2, small.reshape(3, -1), recv_sum


def nodes_body(keep, got1, got2, got3, recv, w1, out):
    share, width = keep.shape
    half = recv.shape[1]
    total = keep[...] + got1[...].astype(F32) + got2[...].astype(F32) + got3[...].astype(F32)
    total_r = recv[...].astype(BF16)
    out[...] = (
        mm(total.astype(BF16), w1[width : 2 * width, :], ((1,), (1,)))
        + mm(total_r[0:share, :], w1[2 * width :, 0:half], ((1,), (1,)))
        + mm(total_r[share:, :], w1[2 * width :, half:], ((1,), (1,)))
    )


def local(node_latents, edge_latents, cotangent, senders, receivers, edge_count, w1, b1, w2, b2, gamma):
    slots, width = edge_latents.shape[2:]
    share = node_latents.shape[0]
    edges = edge_latents.reshape(slots, width)
    cots = cotangent.reshape(slots, width)
    x, z, y, core = [lax.axis_index(name).astype(jnp.int32) for name in ("x", "z", "y", "core")]

    pieces_s = gather_send(node_latents)
    pieces_r = gather_recv(node_latents)

    send = senders.reshape(slots)
    owner, rest = send // share, send % share
    sid = (((owner % NZ - z) % NZ) * NX + (owner // NZ - x) % NX) * share + rest
    recv = receivers.reshape(slots)
    owner, rest = recv // share, recv % share
    rid = (((owner % NCORE - core) % NCORE) * NY + (owner // NCORE - y) % NY) * share + rest
    scalars = jnp.stack([edge_count.reshape(()), core, y])
    place = jnp.stack([x, y, core])

    grad_edges, preb, pay, own_w, own_r, own_small = edge_kernel(
        scalars, sid, rid, edges, cots, w1, w2, b1, b2, gamma, pieces_s, pieces_r
    )
    grad_w1, grad_w2, small, recv_sum = reduce_weights(place, pay, own_w, own_r, own_small)
    send_sum = reduce_send(scatter_kernel(sid, preb, share))
    grad_nodes = call(
        nodes_body, [shaped(share, width, dtype=F32)], [*send_sum, recv_sum, w1], "node_grads", flops=100_000_000
    )[0]
    return (
        grad_edges.reshape(1, 1, slots, width),
        grad_nodes,
        grad_w1,
        small[0],
        grad_w2,
        small[1],
        small[2],
    )


def solution(mesh):
    mesh = Mesh(mesh.devices.reshape(NX, NZ, NY, NCORE), ("x", "z", "y", "core"))
    row, col = ("x", "z"), ("y", "core")
    in_specs = (
        P(col + row, None),
        P(row, col, None, None),
        P(row, col, None, None),
        P(row, col, None),
        P(row, col, None),
        P(row, col),
        P(),
        P(),
        P(),
        P(),
        P(),
    )
    out_specs = (P(row, col, None, None), P(col + row, None), P(), P(), P(), P(), P())
    return jax.shard_map(local, mesh=mesh, in_specs=in_specs, out_specs=out_specs, check_vma=False)
```

```python
import functools

import jax
import jax.numpy as jnp
from jax import lax
from jax.experimental import pallas as pl
from jax.experimental.pallas import tpu as pltpu
from jax.sharding import Mesh, PartitionSpec as P

EPS = 1e-05
NX, NZ, NY, NCORE = 4, 8, 4, 2
BF16 = jnp.bfloat16
F32 = jnp.float32


def shift(value, axis, size, step):
    return lax.ppermute(value, axis, [(i, (i - step) % size) for i in range(size)])


def push(value, axis, size, step):
    return lax.ppermute(value, axis, [(i, (i + step) % size) for i in range(size)])


def swap(value, step, first):
    pairs = []
    for x in range(NX):
        for y in range(NY):
            for core in range(NCORE):
                to = (x, (y + step) % NY) if (core == 0) == first else ((x + step) % NX, y)
                pairs.append(((x * NY + y) * NCORE + core, (to[0] * NY + to[1]) * NCORE + core))
    return lax.ppermute(value, ("x", "y", "core"), pairs)


def stack_body(own, got1, got2, got3, out, again):
    for d, ref in enumerate((own, got1, got2, got3)):
        out[d] = ref[...]
    again[...] = own[...]


def gather(own):
    gots = [shift(own, "x", NX, d) for d in (1, 2, 3)]
    along_x, own = call(stack_body, [shaped(NX, *own.shape), shaped(*own.shape)], [own, *gots], "stack_x")
    a = {0: along_x}
    for d in (1, 2, 3):
        a[d] = shift(a[d - 1], "z", NZ, 1)
        a[NZ - d] = shift(a[(NZ - d + 1) % NZ], "z", NZ, -1)
    a4_lo = shift(a[3][:2], "z", NZ, 1)
    a4_hi = shift(a[5][2:], "z", NZ, -1)
    along_y = jnp.stack([own] + [shift(own, "y", NY, d) for d in (1, 2, 3)])
    pieces_s = [a[0], a[1], a[2], a[3], a4_lo, a4_hi, a[5], a[6], a[7]]
    return pieces_s, [along_y, shift(along_y, "core", NCORE, 1)]


PLACES = [(0, 0, 4), (1, 0, 4), (2, 0, 4), (3, 0, 4), (4, 0, 2), (4, 2, 2), (5, 0, 4), (6, 0, 4), (7, 0, 4)]
SMALL = 16


def mm(a, b, dims):
    return lax.dot_general(a, b, ((dims[0], dims[1]), ((), ())), preferred_element_type=F32)


def one_hot(hit):
    return jnp.where(hit, 1.0, 0.0).astype(BF16)


def split_rows(values):
    high = values.astype(BF16).astype(F32)
    return jnp.concatenate([high, values - high, jnp.zeros((4, values.shape[1]), F32)], axis=0).astype(BF16)


def join_rows(rows):
    rows = rows.astype(F32)
    return rows[0:6] + rows[6:12]


def call(body, out_shape, args, name, scalars=(), scratch=(), flops=1_000_000, where=None, to=None, aliases=None, limit=24):
    vmem = pl.BlockSpec(memory_space=pltpu.VMEM)
    bytes_accessed = sum(a.size * a.dtype.itemsize for a in list(args) + list(out_shape))
    return pl.pallas_call(
        body,
        out_shape=out_shape,
        in_specs=[pl.BlockSpec(memory_space=pltpu.SMEM)] * len(scalars) + (where or [vmem] * len(args)),
        out_specs=to or [vmem] * len(out_shape),
        scratch_shapes=list(scratch),
        input_output_aliases=aliases or {},
        compiler_params=pltpu.CompilerParams(vmem_limit_bytes=limit * 2**20),
        cost_estimate=pl.CostEstimate(flops=flops, bytes_accessed=bytes_accessed, transcendentals=0),
        name=name,
    )(*scalars, *args)


def shaped(*shape, dtype=BF16):
    return jax.ShapeDtypeStruct(shape, dtype)


def owner_of(ids, share):
    scale = (1 << 22) // share + 1
    owner = jnp.right_shift(ids * scale, 22)
    return owner, ids - owner * share


def send_place(ids, scalars, share):
    owner, rest = owner_of(ids, share)
    dz = (owner - scalars[4]) & (NZ - 1)
    dx = (jnp.right_shift(owner, 3) - scalars[3]) & (NX - 1)
    return (dz * NX + dx) * share + rest


def recv_place(ids, scalars, share):
    owner, rest = owner_of(ids, share)
    dcore = (owner - scalars[1]) & (NCORE - 1)
    dy = (jnp.right_shift(owner, 1) - scalars[2]) & (NY - 1)
    return (dcore * NY + dy) * share + rest


def columns(ids, out):
    turned = jnp.transpose(ids)
    lanes = ids.shape[1]
    for j in range(ids.shape[0]):
        out[j * lanes : (j + 1) * lanes, :] = turned[:, j : j + 1]


def edge_kernel_body(tile, scalars, *refs):
    send_ids, recv_ids, recv_row, b1, b2, gamma = refs[:6]
    edges_hbm, cots_hbm, w1_hbm, w2_hbm = refs[6:10]
    pieces_s, pieces_r = refs[10:19], refs[19:21]
    grad_edges_hbm, preb_hbm, pay_hbm, own_w, own_r, own_small = refs[21:27]
    lat_s, lat_r, lefts, cots, w1, w2, rights, grad_edges, pay, sid_col, rid_col, sems, out_sems = refs[27:]
    count, core, x, y = scalars[0], scalars[1], scalars[3], scalars[2]
    slots, width = cots.shape
    half = width // 2
    share = lat_s.shape[2]
    nodes = NZ * NX * share
    block = NCORE * NY * share
    edges, x_s, x_r, activ = [lefts.at[i] for i in range(4)]
    preb, goutb = rights.at[0], rights.at[1]
    started = []

    def send_out(src, dst):
        copy = pltpu.make_async_copy(src, dst, out_sems.at[len(started)])
        copy.start()
        started.append(copy)

    copies = [(ref, lat_r.at[pl.ds(i * NY, NY)]) for i, ref in enumerate(pieces_r)]
    copies += [(ref, lat_s.at[dz, pl.ds(dx, n)]) for ref, (dz, dx, n) in zip(pieces_s, PLACES)]
    copies += [(w1_hbm, w1), (edges_hbm, edges), (w2_hbm, w2), (cots_hbm, cots)]
    copies = [pltpu.make_async_copy(src, dst, sems.at[i]) for i, (src, dst) in enumerate(copies)]
    for copy in copies:
        copy.start()
    columns(send_place(send_ids[...], scalars, share), sid_col)
    columns(recv_place(recv_ids[...], scalars, share), rid_col)
    zero = jnp.zeros((1, width), F32)
    sum_b1, sum_b2, sum_gain = zero, zero, zero
    for t in range(slots // tile):
        rows = slice(t * tile, (t + 1) * tile)
        hot_r = one_hot(rid_col[rows, :] == lax.broadcasted_iota(jnp.int32, (tile, block), 1))
        hot_s = one_hot(sid_col[rows, :] == lax.broadcasted_iota(jnp.int32, (tile, nodes), 1))
        if t == 0:
            for copy in copies[:11]:
                copy.wait()
        xr = mm(hot_r, lat_r[...].reshape(block, width), ((1,), (0,))).astype(BF16)
        xs = mm(hot_s, lat_s[...].reshape(nodes, width), ((1,), (0,))).astype(BF16)
        x_s[rows, :] = xs
        x_r[rows, :] = xr
        if t == 0:
            for copy in copies[11:13]:
                copy.wait()
        pre = (
            mm(xr, w1[2 * width :, :], ((1,), (0,)))
            + mm(xs, w1[width : 2 * width, :], ((1,), (0,)))
            + mm(edges[rows, :], w1[0:width, :], ((1,), (0,)))
            + b1[...]
        )
        sigma = jax.nn.sigmoid(pre)
        act = (pre * sigma).astype(BF16)
        slope = sigma * (1.0 + pre * (1.0 - sigma))
        activ[rows, :] = act
        if t == 0:
            for copy in copies[13:]:
                copy.wait()
        output = mm(act, w2[...], ((1,), (0,))) + b2[...]
        centred = output - jnp.mean(output, axis=1, keepdims=True)
        inv_std = lax.rsqrt(jnp.mean(centred * centred, axis=1, keepdims=True) + EPS)
        normed = centred * inv_std
        live = t * tile + lax.broadcasted_iota(jnp.int32, (tile, 1), 0) < count
        g = jnp.where(live, cots[rows, :].astype(F32), 0.0)
        sum_gain = sum_gain + jnp.sum(g * normed, axis=0, keepdims=True)
        grad_norm = g * gamma[...]
        grad_out = inv_std * (
            grad_norm
            - jnp.mean(grad_norm, axis=1, keepdims=True)
            - normed * jnp.mean(grad_norm * normed, axis=1, keepdims=True)
        )
        gob = grad_out.astype(BF16)
        goutb[rows, :] = gob
        sum_b2 = sum_b2 + jnp.sum(grad_out, axis=0, keepdims=True)
        grad_pre = mm(gob, w2[...], ((1,), (1,))) * slope
        sum_b1 = sum_b1 + jnp.sum(grad_pre, axis=0, keepdims=True)
        gpb = grad_pre.astype(BF16)
        preb[rows, :] = gpb
        grad_edges[rows, :] = (g + mm(gpb, w1[0:width, :], ((1,), (1,)))).astype(BF16)
    send_out(preb, preb_hbm)
    send_out(grad_edges, grad_edges_hbm)

    first = NY * width
    rid_row = recv_place(recv_row[...], scalars, share)
    for core_at in range(NCORE):
        ids = core_at * NY * share + lax.broadcasted_iota(jnp.int32, (NY * share, slots), 0)
        sums_r = mm(one_hot(rid_row == ids), preb[...], ((1,), (0,)))
        for d in range(NY):
            for h in range(2):
                part = sums_r[d * share : (d + 1) * share, h * half : (h + 1) * half]
                at = (2 * d + h) * share
                if core_at == 0:
                    own_r[at : at + share, :] = part
                else:
                    pay[first + at : first + at + share, :] = part.astype(BF16)
    parts = [s[:, h * half : (h + 1) * half] for s in (sum_b1, sum_b2, sum_gain) for h in range(2)]
    small = split_rows(jnp.concatenate(parts, axis=0))
    own_small[...] = small
    at = first + 2 * NY * share
    pay[at : at + SMALL, :] = small
    send_out(pay.at[pl.ds(first, at + SMALL - first)], pay_hbm.at[pl.ds(first, at + SMALL - first)])

    own = pl.ds(pl.multiple_of(core * half, half), half)
    peer = pl.ds(pl.multiple_of((1 - core) * half, half), half)
    mine = jnp.where(core == 0, y, x)
    others = jnp.where(core == 0, x, y)
    for cols, axis_at, ref, hbm in ((peer, others, pay, pay_hbm), (own, mine, own_w, None)):
        for d in range(NY):
            i = (axis_at + d) & (NY - 1)
            right = jnp.where(i == NY - 1, 1, 0)
            rows = pl.ds(d * width, width)
            ref[rows, :] = mm(lefts[i], rights[right, :, cols], ((0,), (0,))).astype(ref.dtype)
            if hbm is not None:
                send_out(ref.at[rows], hbm.at[rows])
    for copy in started:
        copy.wait()


def edge_kernel(scalars, senders, receivers, edges, cots, w1, w2, b1, b2, gamma, pieces_s, pieces_r):
    slots, width = edges.shape
    half = width // 2
    share = pieces_s[0].shape[1]
    vmem = pl.BlockSpec(memory_space=pltpu.VMEM)
    hbm = pl.BlockSpec(memory_space=pl.ANY)
    recv_rows = 2 * NY * share
    out_shape = [
        shaped(slots, width),
        shaped(slots, width),
        shaped(NY * width + recv_rows + SMALL, half),
        shaped(NY * width, half, dtype=F32),
        shaped(recv_rows, half, dtype=F32),
        shaped(SMALL, half),
    ]
    return call(
        functools.partial(edge_kernel_body, 256),
        out_shape,
        [
            senders.reshape(-1, 128),
            receivers.reshape(-1, 128),
            receivers.reshape(1, slots),
            b1.reshape(1, width),
            b2.reshape(1, width),
            gamma.reshape(1, width),
            edges,
            cots,
            w1,
            w2,
            *pieces_s,
            *pieces_r,
        ],
        "edge_step",
        scalars=[scalars],
        where=[vmem] * 6 + [hbm] * 15,
        to=[hbm] * 3 + [vmem] * 3,
        scratch=[
            pltpu.VMEM((NZ, NX, share, width), BF16),
            pltpu.VMEM((NCORE * NY, share, width), BF16),
            pltpu.VMEM((4, slots, width), BF16),
            pltpu.VMEM((slots, width), BF16),
            pltpu.VMEM(w1.shape, BF16),
            pltpu.VMEM(w2.shape, BF16),
            pltpu.VMEM((2, slots, width), BF16),
            pltpu.VMEM((slots, width), BF16),
            pltpu.VMEM(out_shape[2].shape, BF16),
            pltpu.VMEM((slots, 1), jnp.int32),
            pltpu.VMEM((slots, 1), jnp.int32),
            pltpu.SemaphoreType.DMA((15,)),
            pltpu.SemaphoreType.DMA((12,)),
        ],
        flops=10_000_000_000,
        limit=56,
    )


def scatter_body(scalars, send_row, preb, *outs):
    slots, width = preb.shape
    share = outs[0].shape[1]
    grads = preb[...]
    sid_row = send_place(send_row[...], scalars, share)
    for ref, (dz, dx, n) in zip(outs, PLACES):
        first = (dz * NX + dx) * share
        hit = sid_row == first + lax.broadcasted_iota(jnp.int32, (n * share, slots), 0)
        ref[...] = mm(one_hot(hit), grads, ((1,), (0,))).astype(BF16).reshape(n, share, width)


def scatter_kernel(scalars, senders, preb, share):
    slots, width = preb.shape
    out_shape = [shaped(n, share, width) for _, _, n in PLACES]
    args = [senders.reshape(1, slots), preb]
    return call(scatter_body, out_shape, args, "scatter", scalars=[scalars], flops=3_000_000_000, limit=48)


def add_pair(pairs):
    for mine, got, out, first in pairs:
        n, size = got.shape[0], mine.shape[0]
        out[first : first + n] = (mine[first : first + n].astype(F32) + got[...].astype(F32)).astype(BF16)
        if first > 0:
            out[0:first] = mine[0:first]
        if first + n < size:
            out[first + n : size] = mine[first + n : size]


def first_add_body(up, got_up, down, got_down, after, out_up, out_down):
    add_pair([(up, got_up, out_up, 0), (down, got_down, out_down, 2)])


def turn(mine, up, down, keep, sends):
    total = mine[...].astype(F32) + up[...].astype(F32) + down[...].astype(F32)
    keep[...] = total[0]
    for d, ref in enumerate(sends):
        ref[...] = total[d + 1].astype(BF16)


def core_body(own_w, own_r, own_small, got, after, keep, small, keep_r, r_all, *refs):
    sends, (staged, sem) = refs[:3], refs[3:]
    rows, recv = own_w.shape[0] // NY, own_r.shape[0] // NY
    first = own_w.shape[0]
    at = first + own_r.shape[0]
    for d in range(NY):
        total_r = own_r[d * recv : (d + 1) * recv, :] + got[first + d * recv : first + (d + 1) * recv, :].astype(F32)
        if d == 0:
            keep_r[...] = total_r
        else:
            staged[d - 1] = total_r.astype(BF16)
    copy = pltpu.make_async_copy(staged, r_all, sem)
    copy.start()
    summed = split_rows(join_rows(own_small[...]) + join_rows(got[at : at + SMALL, :]))
    small[...] = summed
    for d in range(NY):
        total_w = own_w[d * rows : (d + 1) * rows, :] + got[d * rows : (d + 1) * rows, :].astype(F32)
        if d == 0:
            keep[...] = total_w
        else:
            ref = sends[d - 1]
            ref[0:rows, :] = total_w.astype(BF16)
            ref[rows : rows + SMALL, :] = summed
    copy.wait()


def add_smalls(smalls, own, gots, me, size):
    smalls[me] = own
    for d, got in enumerate(gots):
        smalls[lax.rem(me + size - 1 - d, size)] = got
    total = join_rows(smalls[0])
    for i in range(1, size):
        total = total + join_rows(smalls[i])
    return split_rows(total)


def first_body(place, keep, small, got1, got2, got3, keep_2, small_2, send1, send2, send3, total, smalls):
    me, next_me = place[0], place[1]
    n = keep.shape[0]
    summed = keep[...]
    for got in (got1, got2, got3):
        summed = summed + got[0:n, :].astype(F32)
    total[...] = summed
    small_2[...] = add_smalls(smalls, small[...], [got[n : n + SMALL, :] for got in (got1, got2, got3)], me, NY)
    part = n // NX
    keep_2[...] = total[pl.ds(pl.multiple_of(next_me * part, part), part), :]
    for d, ref in ((1, send1), (2, send2), (3, send3)):
        at = pl.multiple_of(((next_me + d) & (NX - 1)) * part, part)
        ref[0:part, :] = total[pl.ds(at, part), :].astype(BF16)
        ref[part : part + SMALL, :] = small_2[...]


def second_body(
    place, keep, small, got1, got2, got3, up, got_up, down, got_down, r_all, out, out_up, out_down, r1, smalls, sem
):
    copy = pltpu.make_async_copy(r_all.at[0], r1, sem)
    copy.start()
    gots = (got1, got2, got3)
    n = keep.shape[0]
    summed = keep[...]
    for got in gots:
        summed = summed + got[0:n, :].astype(F32)
    out[0:n, :] = summed.astype(BF16)
    out[n : n + SMALL, :] = add_smalls(smalls, small[...], [got[n : n + SMALL, :] for got in gots], place[1], NX)
    add_pair([(up, got_up, out_up, 0), (down, got_down, out_down, 0)])
    copy.wait()


def merge(a, b, out):
    n = a.shape[0] - SMALL
    out[0:n, :] = (a[0:n, :].astype(F32) + b[0:n, :].astype(F32)).astype(BF16)
    out[n : n + SMALL, :] = split_rows(join_rows(a[n : n + SMALL, :]) + join_rows(b[n : n + SMALL, :]))


def merge_body(a, b, r_all, out, r2, sem):
    copy = pltpu.make_async_copy(r_all.at[1], r2, sem)
    copy.start()
    merge(a, b, out)
    copy.wait()


def merge_add_body(a, b, up, got_up, down, got_down, r_all, keep_r, got_r1, out, out_up, out_down, r3, total_r, sem):
    copy = pltpu.make_async_copy(r_all.at[2], r3, sem)
    copy.start()
    merge(a, b, out)
    add_pair([(up, got_up, out_up, 0), (down, got_down, out_down, 0)])
    total_r[...] = keep_r[...] + got_r1[...].astype(F32)
    copy.wait()


def last_merge_body(a, b, keep_r, got_r2, out, small, total_r):
    n = a.shape[0] - SMALL
    out[...] = (a[0:n, :].astype(F32) + b[0:n, :].astype(F32)).astype(BF16)
    small[...] = split_rows(join_rows(a[n : n + SMALL, :]) + join_rows(b[n : n + SMALL, :]))
    total_r[...] = keep_r[...] + got_r2[...].astype(F32)


def lay_part_body(place, own, got1, got2, got3, mine, up, down, keep_r, got_r3, out, total_r, keep, *sends):
    n = own.shape[0]
    for d, ref in enumerate((own, got1, got2, got3)):
        at = pl.multiple_of(((place[1] + d) & (NX - 1)) * n, n)
        out[pl.ds(at, n), :] = ref[...]
    total_r[...] = keep_r[...] + got_r3[...].astype(F32)
    turn(mine, up, down, keep, sends)


def stack_weights_body(own, got1, got2, got3, small, keep, send1, send2, send3, recv, w1, out, grad_nodes):
    n = own.shape[0]
    for d, ref in enumerate((own, got1, got2, got3)):
        out[d * n : (d + 1) * n, :] = ref[...]
    out[NY * n :, :] = small[...]
    nodes(keep, send1, send2, send3, recv, w1, grad_nodes)


def lay_half_body(place, pieces, *refs):
    laid, sems = refs[-2:]
    n, half = laid.shape[1:]
    if len(refs) > 4:
        mine, (grad_w1, grad_w2, *smalls) = refs[2], refs[3:8]
        other = join_rows(pieces[NY * n : NY * n + SMALL, :])
        small = jnp.where(place[1] == 0, other, join_rows(mine[...]))
        for i, ref in enumerate(smalls):
            for h in range(2):
                ref[:, h * half : (h + 1) * half] = small[2 * i + h : 2 * i + h + 1, :]
    else:
        grad_w1, grad_w2 = refs[:2]
    cols = pl.ds(pl.multiple_of(place[1] * half, half), half)
    for d in range(NY):
        i = (place[0] + d) & (NY - 1)
        laid[d] = pieces[d * n : (d + 1) * n, :].astype(F32)

        @pl.when(i < NY - 1)
        def _():
            rows = pl.ds(pl.multiple_of(i * n, n), n)
            pltpu.make_async_copy(laid.at[d], grad_w1.at[rows, cols], sems.at[d]).start()

        @pl.when(i == NY - 1)
        def _():
            pltpu.make_async_copy(laid.at[d], grad_w2.at[:, cols], sems.at[d]).start()

    for d in range(NY):
        pltpu.make_async_copy(laid.at[d], grad_w2.at[:, pl.ds(0, half)], sems.at[d]).wait()


def lay_half(place, pieces, rows, so_far=()):
    half = pieces.shape[1]
    vmem = pl.BlockSpec(memory_space=pltpu.VMEM)
    hbm = pl.BlockSpec(memory_space=pl.ANY)
    out_shape = [shaped((NY - 1) * rows, 2 * half, dtype=F32), shaped(rows, 2 * half, dtype=F32)]
    out_shape += [shaped(1, 2 * half, dtype=F32)] * 3 if so_far else []
    return call(
        lay_half_body,
        out_shape,
        [pieces, *so_far],
        "lay_half",
        scalars=[place],
        where=[vmem] + ([hbm, hbm, vmem] if so_far else []),
        to=[hbm, hbm] + ([vmem] * 3 if so_far else []),
        scratch=[pltpu.VMEM((NY, rows, half), F32), pltpu.SemaphoreType.DMA((NY,))],
        aliases={2: 0, 3: 1} if so_far else {},
    )


def z_ring(up, down):
    return push(up, "z", NZ, 1), push(down, "z", NZ, -1)


def flip(value, bit):
    return lax.ppermute(value, "z", [(i, i ^ bit) for i in range(NZ)])


def reduce_all(place, pay, own_w, own_r, own_small, pieces, w1):
    a0, a1, a2, a3, a4_lo, a4_hi, a5, a6, a7 = pieces
    share, width = a0.shape[1:]
    ring = [shaped(*a0.shape)] * 2
    half = pay.shape[1]
    rows, recv = own_w.shape[0] // NY, own_r.shape[0] // NY
    sum_r, part_r = shaped(recv, half, dtype=F32), shaped(recv, half)
    vmem = pl.BlockSpec(memory_space=pltpu.VMEM)
    hbm = pl.BlockSpec(memory_space=pl.ANY)
    dma = pltpu.SemaphoreType.DMA

    got = push(pay, "core", NCORE, 1)
    got_up, got_down = z_ring(a4_lo, a4_hi)
    out_shape = [shaped(rows, half, dtype=F32), shaped(SMALL, half), sum_r, shaped(3, recv, half)]
    keep, small, keep_r, r_all, *sends = call(
        core_body,
        out_shape + [shaped(rows + SMALL, half)] * 3,
        [own_w, own_r, own_small, got, a4_lo],
        "after_core",
        to=[vmem] * 3 + [hbm] + [vmem] * 3,
        scratch=[pltpu.VMEM((3, recv, half), BF16), dma],
    )
    gots = [swap(part, d + 1, True) for d, part in enumerate(sends)]
    up, down = call(first_add_body, ring, [a3, got_up, a5, got_down, small], "first_add")
    got_up, got_down = z_ring(up, down)

    part = rows // NX
    out_shape = [shaped(part, half, dtype=F32), shaped(SMALL, half)] + [shaped(part + SMALL, half)] * 3
    keep, small, *sends = call(
        first_body,
        out_shape,
        [keep, small, *gots],
        "after_first",
        scalars=[place],
        scratch=[pltpu.VMEM((rows, half), F32), pltpu.VMEM((NY, SMALL, half), BF16)],
    )
    gots = [swap(part, d + 1, False) for d, part in enumerate(sends)]
    payload = shaped(part + SMALL, half)
    value, up, down, r1 = call(
        second_body,
        [payload] + ring + [part_r],
        [keep, small, *gots, a2, got_up, a6, got_down, r_all],
        "after_second",
        scalars=[place],
        where=[vmem] * 9 + [hbm],
        scratch=[pltpu.VMEM((NX, SMALL, half), BF16), dma],
    )
    got_up, got_down = z_ring(up, down)
    got_r1 = push(r1, "y", NY, 1)
    value, r2 = call(
        merge_body, [payload, part_r], [value, flip(value, 1), r_all], "merge_1", where=[vmem] * 2 + [hbm], scratch=[dma]
    )
    got_r2 = push(r2, "y", NY, 2)
    value, up, down, r3, keep_r = call(
        merge_add_body,
        [payload] + ring + [part_r, sum_r],
        [value, flip(value, 2), a1, got_up, a7, got_down, r_all, keep_r, got_r1],
        "merge_2",
        where=[vmem] * 6 + [hbm] + [vmem] * 2,
        scratch=[dma],
    )
    got_up, got_down = z_ring(up, down)
    got_r3 = push(r3, "y", NY, 3)
    value, small, keep_r = call(
        last_merge_body,
        [shaped(part, half), shaped(SMALL, half), sum_r],
        [value, flip(value, 4), keep_r, got_r2],
        "merge_4",
    )
    gots = [swap(value, -d, False) for d in (1, 2, 3)]
    out_shape = [shaped(rows, half), sum_r, shaped(share, width, dtype=F32)] + [shaped(share, width)] * 3
    value, recv_sum, keep, *sends = call(
        lay_part_body,
        out_shape,
        [value, *gots, a0, got_up, got_down, keep_r, got_r3],
        "lay_part",
        scalars=[place],
    )
    gots = [swap(value, -d, True) for d in (1, 2, 3)]
    send_sum = [keep] + [push(part, "x", NX, d + 1) for d, part in enumerate(sends)]
    mine, grad_nodes = call(
        stack_weights_body,
        [shaped(NY * rows + SMALL, half), shaped(share, width, dtype=F32)],
        [value, *gots, small, *send_sum, recv_sum, w1],
        "stack_weights",
        flops=100_000_000,
    )
    other = push(mine, "core", NCORE, 1)
    core = place[2]
    laid = lay_half(jnp.stack([place[0], core]), mine, rows)
    grad_w1, grad_w2, *small = lay_half(jnp.stack([place[1], 1 - core]), other, rows, [*laid, mine[NY * rows :]])
    return grad_w1, grad_w2, [s.reshape(-1) for s in small], grad_nodes


def nodes(keep, got1, got2, got3, recv, w1, out):
    share, width = keep.shape
    half = recv.shape[1]
    total = keep[...] + got1[...].astype(F32) + got2[...].astype(F32) + got3[...].astype(F32)
    total_r = recv[...].astype(BF16)
    out[...] = (
        mm(total.astype(BF16), w1[width : 2 * width, :], ((1,), (1,)))
        + mm(total_r[0:share, :], w1[2 * width :, 0:half], ((1,), (1,)))
        + mm(total_r[share:, :], w1[2 * width :, half:], ((1,), (1,)))
    )


def local(node_latents, edge_latents, cotangent, senders, receivers, edge_count, w1, b1, w2, b2, gamma):
    slots, width = edge_latents.shape[2:]
    share = node_latents.shape[0]
    edges = edge_latents.reshape(slots, width)
    cots = cotangent.reshape(slots, width)
    x, z, y, core = [lax.axis_index(name).astype(jnp.int32) for name in ("x", "z", "y", "core")]
    scalars = jnp.stack([edge_count.reshape(()), core, y, x, z])
    place = jnp.stack([jnp.where(core == 0, y, x), jnp.where(core == 0, x, y), core])

    pieces_s, pieces_r = gather(node_latents)
    grad_edges, preb, pay, own_w, own_r, own_small = edge_kernel(
        scalars, senders, receivers, edges, cots, w1, w2, b1, b2, gamma, pieces_s, pieces_r
    )
    sums = scatter_kernel(scalars, senders, preb, share)
    grad_w1, grad_w2, small, grad_nodes = reduce_all(place, pay, own_w, own_r, own_small, sums, w1)
    return (
        grad_edges.reshape(1, 1, slots, width),
        grad_nodes,
        grad_w1,
        small[0],
        grad_w2,
        small[1],
        small[2],
    )


def solution(mesh):
    mesh = Mesh(mesh.devices.reshape(NX, NZ, NY, NCORE), ("x", "z", "y", "core"))
    row, col = ("x", "z"), ("y", "core")
    in_specs = (
        P(col + row, None),
        P(row, col, None, None),
        P(row, col, None, None),
        P(row, col, None),
        P(row, col, None),
        P(row, col),
        P(),
        P(),
        P(),
        P(),
        P(),
    )
    out_specs = (P(row, col, None, None), P(col + row, None), P(), P(), P(), P(), P())
    return jax.shard_map(local, mesh=mesh, in_specs=in_specs, out_specs=out_specs, check_vma=False)
```

```python
import functools

import jax
import jax.numpy as jnp
from jax import lax
from jax.experimental import pallas as pl
from jax.experimental.pallas import tpu as pltpu
from jax.sharding import Mesh, PartitionSpec as P

EPS = 1e-05
NX, NZ, NY, NCORE = 4, 8, 4, 2
BF16 = jnp.bfloat16
F32 = jnp.float32


def shift(value, axis, size, step):
    return lax.ppermute(value, axis, [(i, (i - step) % size) for i in range(size)])


def push(value, axis, size, step):
    return lax.ppermute(value, axis, [(i, (i + step) % size) for i in range(size)])


def swap(value, step, first):
    pairs = []
    for x in range(NX):
        for y in range(NY):
            for core in range(NCORE):
                to = (x, (y + step) % NY) if (core == 0) == first else ((x + step) % NX, y)
                pairs.append(((x * NY + y) * NCORE + core, (to[0] * NY + to[1]) * NCORE + core))
    return lax.ppermute(value, ("x", "y", "core"), pairs)


def stack_body(own, got1, got2, got3, out, again):
    for d, ref in enumerate((own, got1, got2, got3)):
        out[d] = ref[...]
    again[...] = own[...]


def gather(own):
    gots = [shift(own, "x", NX, d) for d in (1, 2, 3)]
    along_x, own = call(stack_body, [shaped(NX, *own.shape), shaped(*own.shape)], [own, *gots], "stack_x")
    a = {0: along_x}
    for d in (1, 2, 3):
        a[d] = shift(a[d - 1], "z", NZ, 1)
        a[NZ - d] = shift(a[(NZ - d + 1) % NZ], "z", NZ, -1)
    a4_lo = shift(a[3][:2], "z", NZ, 1)
    a4_hi = shift(a[5][2:], "z", NZ, -1)
    along_y = jnp.stack([own] + [shift(own, "y", NY, d) for d in (1, 2, 3)])
    pieces_s = [a[0], a[1], a[2], a[3], a4_lo, a4_hi, a[5], a[6], a[7]]
    return pieces_s, [along_y, shift(along_y, "core", NCORE, 1)]


PLACES = [(0, 0, 4), (1, 0, 4), (2, 0, 4), (3, 0, 4), (4, 0, 2), (4, 2, 2), (5, 0, 4), (6, 0, 4), (7, 0, 4)]
SMALL = 16


def mm(a, b, dims):
    return lax.dot_general(a, b, ((dims[0], dims[1]), ((), ())), preferred_element_type=F32)


def one_hot(hit):
    return jnp.where(hit, 1.0, 0.0).astype(BF16)


def split_rows(values):
    high = values.astype(BF16).astype(F32)
    return jnp.concatenate([high, values - high, jnp.zeros((4, values.shape[1]), F32)], axis=0).astype(BF16)


def join_rows(rows):
    rows = rows.astype(F32)
    return rows[0:6] + rows[6:12]


def call(body, out_shape, args, name, scalars=(), scratch=(), flops=1_000_000, where=None, to=None, aliases=None, limit=24):
    vmem = pl.BlockSpec(memory_space=pltpu.VMEM)
    bytes_accessed = sum(a.size * a.dtype.itemsize for a in list(args) + list(out_shape))
    return pl.pallas_call(
        body,
        out_shape=out_shape,
        in_specs=[pl.BlockSpec(memory_space=pltpu.SMEM)] * len(scalars) + (where or [vmem] * len(args)),
        out_specs=to or [vmem] * len(out_shape),
        scratch_shapes=list(scratch),
        input_output_aliases=aliases or {},
        compiler_params=pltpu.CompilerParams(vmem_limit_bytes=limit * 2**20),
        cost_estimate=pl.CostEstimate(flops=flops, bytes_accessed=bytes_accessed, transcendentals=0),
        name=name,
    )(*scalars, *args)


def shaped(*shape, dtype=BF16):
    return jax.ShapeDtypeStruct(shape, dtype)


def owner_of(ids, share):
    scale = (1 << 22) // share + 1
    owner = jnp.right_shift(ids * scale, 22)
    return owner, ids - owner * share


def send_place(ids, scalars, share):
    owner, rest = owner_of(ids, share)
    dz = (owner - scalars[4]) & (NZ - 1)
    dx = (jnp.right_shift(owner, 3) - scalars[3]) & (NX - 1)
    return (dz * NX + dx) * share + rest


def recv_place(ids, scalars, share):
    owner, rest = owner_of(ids, share)
    dcore = (owner - scalars[1]) & (NCORE - 1)
    dy = (jnp.right_shift(owner, 1) - scalars[2]) & (NY - 1)
    return (dcore * NY + dy) * share + rest


def columns(ids, out):
    turned = jnp.transpose(ids)
    lanes = ids.shape[1]
    for j in range(ids.shape[0]):
        out[j * lanes : (j + 1) * lanes, :] = turned[:, j : j + 1]


def edge_kernel_body(tile, scalars, *refs):
    send_ids, recv_ids, recv_row, b1, b2, gamma = refs[:6]
    edges_hbm, cots_hbm, w1_hbm, w2_hbm = refs[6:10]
    pieces_s, pieces_r = refs[10:19], refs[19:21]
    grad_edges_hbm, preb_hbm, pay_hbm, own_w, own_r, own_small = refs[21:27]
    lat_s, lat_r, lefts, cots, w1, w2, rights, grad_edges, pay, sid_col, rid_col, sems, out_sems = refs[27:]
    count, core, x, y = scalars[0], scalars[1], scalars[3], scalars[2]
    slots, width = cots.shape
    half = width // 2
    share = lat_s.shape[2]
    nodes = NZ * NX * share
    block = NCORE * NY * share
    edges, x_s, x_r, activ = [lefts.at[i] for i in range(4)]
    preb, goutb = rights.at[0], rights.at[1]
    started = []

    def send_out(src, dst):
        copy = pltpu.make_async_copy(src, dst, out_sems.at[len(started)])
        copy.start()
        started.append(copy)

    copies = [(ref, lat_r.at[pl.ds(i * NY, NY)]) for i, ref in enumerate(pieces_r)]
    copies += [(ref, lat_s.at[dz, pl.ds(dx, n)]) for ref, (dz, dx, n) in zip(pieces_s, PLACES)]
    copies += [(w1_hbm, w1), (edges_hbm, edges), (w2_hbm, w2), (cots_hbm, cots)]
    copies = [pltpu.make_async_copy(src, dst, sems.at[i]) for i, (src, dst) in enumerate(copies)]
    for copy in copies:
        copy.start()
    columns(send_place(send_ids[...], scalars, share), sid_col)
    columns(recv_place(recv_ids[...], scalars, share), rid_col)
    zero = jnp.zeros((1, width), F32)
    sum_b1, sum_b2, sum_gain = zero, zero, zero
    for t in range(slots // tile):
        rows = slice(t * tile, (t + 1) * tile)
        hot_r = one_hot(rid_col[rows, :] == lax.broadcasted_iota(jnp.int32, (tile, block), 1))
        hot_s = one_hot(sid_col[rows, :] == lax.broadcasted_iota(jnp.int32, (tile, nodes), 1))
        if t == 0:
            for copy in copies[:11]:
                copy.wait()
        xr = mm(hot_r, lat_r[...].reshape(block, width), ((1,), (0,))).astype(BF16)
        xs = mm(hot_s, lat_s[...].reshape(nodes, width), ((1,), (0,))).astype(BF16)
        x_s[rows, :] = xs
        x_r[rows, :] = xr
        if t == 0:
            for copy in copies[11:13]:
                copy.wait()
        pre = (
            mm(xr, w1[2 * width :, :], ((1,), (0,)))
            + mm(xs, w1[width : 2 * width, :], ((1,), (0,)))
            + mm(edges[rows, :], w1[0:width, :], ((1,), (0,)))
            + b1[...]
        )
        sigma = jax.nn.sigmoid(pre)
        act = (pre * sigma).astype(BF16)
        slope = sigma * (1.0 + pre * (1.0 - sigma))
        activ[rows, :] = act
        if t == 0:
            for copy in copies[13:]:
                copy.wait()
        output = mm(act, w2[...], ((1,), (0,))) + b2[...]
        centred = output - jnp.mean(output, axis=1, keepdims=True)
        inv_std = lax.rsqrt(jnp.mean(centred * centred, axis=1, keepdims=True) + EPS)
        normed = centred * inv_std
        live = t * tile + lax.broadcasted_iota(jnp.int32, (tile, 1), 0) < count
        g = jnp.where(live, cots[rows, :].astype(F32), 0.0)
        sum_gain = sum_gain + jnp.sum(g * normed, axis=0, keepdims=True)
        grad_norm = g * gamma[...]
        grad_out = inv_std * (
            grad_norm
            - jnp.mean(grad_norm, axis=1, keepdims=True)
            - normed * jnp.mean(grad_norm * normed, axis=1, keepdims=True)
        )
        gob = grad_out.astype(BF16)
        goutb[rows, :] = gob
        sum_b2 = sum_b2 + jnp.sum(grad_out, axis=0, keepdims=True)
        grad_pre = mm(gob, w2[...], ((1,), (1,))) * slope
        sum_b1 = sum_b1 + jnp.sum(grad_pre, axis=0, keepdims=True)
        gpb = grad_pre.astype(BF16)
        preb[rows, :] = gpb
        grad_edges[rows, :] = (g + mm(gpb, w1[0:width, :], ((1,), (1,)))).astype(BF16)
    send_out(preb, preb_hbm)
    send_out(grad_edges, grad_edges_hbm)

    first = NY * width
    rid_row = recv_place(recv_row[...], scalars, share)
    for core_at in range(NCORE):
        ids = core_at * NY * share + lax.broadcasted_iota(jnp.int32, (NY * share, slots), 0)
        sums_r = mm(one_hot(rid_row == ids), preb[...], ((1,), (0,)))
        for d in range(NY):
            for h in range(2):
                part = sums_r[d * share : (d + 1) * share, h * half : (h + 1) * half]
                at = (2 * d + h) * share
                if core_at == 0:
                    own_r[at : at + share, :] = part
                else:
                    pay[first + at : first + at + share, :] = part.astype(BF16)
    parts = [s[:, h * half : (h + 1) * half] for s in (sum_b1, sum_b2, sum_gain) for h in range(2)]
    small = split_rows(jnp.concatenate(parts, axis=0))
    own_small[...] = small
    at = first + 2 * NY * share
    pay[at : at + SMALL, :] = small
    send_out(pay.at[pl.ds(first, at + SMALL - first)], pay_hbm.at[pl.ds(first, at + SMALL - first)])

    own = pl.ds(pl.multiple_of(core * half, half), half)
    peer = pl.ds(pl.multiple_of((1 - core) * half, half), half)
    mine = jnp.where(core == 0, y, x)
    others = jnp.where(core == 0, x, y)
    for cols, axis_at, ref, hbm in ((peer, others, pay, pay_hbm), (own, mine, own_w, None)):
        for d in range(NY):
            i = (axis_at + d) & (NY - 1)
            right = jnp.where(i == NY - 1, 1, 0)
            rows = pl.ds(d * width, width)
            ref[rows, :] = mm(lefts[i], rights[right, :, cols], ((0,), (0,))).astype(ref.dtype)
            if hbm is not None:
                send_out(ref.at[rows], hbm.at[rows])
    for copy in started:
        copy.wait()


def edge_kernel(scalars, senders, receivers, edges, cots, w1, w2, b1, b2, gamma, pieces_s, pieces_r):
    slots, width = edges.shape
    half = width // 2
    share = pieces_s[0].shape[1]
    vmem = pl.BlockSpec(memory_space=pltpu.VMEM)
    hbm = pl.BlockSpec(memory_space=pl.ANY)
    recv_rows = 2 * NY * share
    out_shape = [
        shaped(slots, width),
        shaped(slots, width),
        shaped(NY * width + recv_rows + SMALL, half),
        shaped(NY * width, half, dtype=F32),
        shaped(recv_rows, half, dtype=F32),
        shaped(SMALL, half),
    ]
    return call(
        functools.partial(edge_kernel_body, 1024),
        out_shape,
        [
            senders.reshape(-1, 128),
            receivers.reshape(-1, 128),
            receivers.reshape(1, slots),
            b1.reshape(1, width),
            b2.reshape(1, width),
            gamma.reshape(1, width),
            edges,
            cots,
            w1,
            w2,
            *pieces_s,
            *pieces_r,
        ],
        "edge_step",
        scalars=[scalars],
        where=[vmem] * 6 + [hbm] * 15,
        to=[hbm] * 3 + [vmem] * 3,
        scratch=[
            pltpu.VMEM((NZ, NX, share, width), BF16),
            pltpu.VMEM((NCORE * NY, share, width), BF16),
            pltpu.VMEM((4, slots, width), BF16),
            pltpu.VMEM((slots, width), BF16),
            pltpu.VMEM(w1.shape, BF16),
            pltpu.VMEM(w2.shape, BF16),
            pltpu.VMEM((2, slots, width), BF16),
            pltpu.VMEM((slots, width), BF16),
            pltpu.VMEM(out_shape[2].shape, BF16),
            pltpu.VMEM((slots, 1), jnp.int32),
            pltpu.VMEM((slots, 1), jnp.int32),
            pltpu.SemaphoreType.DMA((15,)),
            pltpu.SemaphoreType.DMA((12,)),
        ],
        flops=10_000_000_000,
        limit=56,
    )


def scatter_body(scalars, send_row, preb, *outs):
    slots, width = preb.shape
    share = outs[0].shape[1]
    grads = preb[...]
    sid_row = send_place(send_row[...], scalars, share)
    for ref, (dz, dx, n) in zip(outs, PLACES):
        first = (dz * NX + dx) * share
        hit = sid_row == first + lax.broadcasted_iota(jnp.int32, (n * share, slots), 0)
        ref[...] = mm(one_hot(hit), grads, ((1,), (0,))).astype(BF16).reshape(n, share, width)


def scatter_kernel(scalars, senders, preb, share):
    slots, width = preb.shape
    out_shape = [shaped(n, share, width) for _, _, n in PLACES]
    args = [senders.reshape(1, slots), preb]
    return call(scatter_body, out_shape, args, "scatter", scalars=[scalars], flops=3_000_000_000, limit=48)


def add_pair(pairs):
    for mine, got, out, first in pairs:
        n, size = got.shape[0], mine.shape[0]
        out[first : first + n] = (mine[first : first + n].astype(F32) + got[...].astype(F32)).astype(BF16)
        if first > 0:
            out[0:first] = mine[0:first]
        if first + n < size:
            out[first + n : size] = mine[first + n : size]


def first_add_body(up, got_up, down, got_down, after, out_up, out_down):
    add_pair([(up, got_up, out_up, 0), (down, got_down, out_down, 2)])


def turn(mine, up, down, keep, sends):
    total = mine[...].astype(F32) + up[...].astype(F32) + down[...].astype(F32)
    keep[...] = total[0]
    for d, ref in enumerate(sends):
        ref[...] = total[d + 1].astype(BF16)


def core_body(own_w, own_r, own_small, got, after, keep, small, keep_r, r_all, *refs):
    sends, (staged, sem) = refs[:3], refs[3:]
    rows, recv = own_w.shape[0] // NY, own_r.shape[0] // NY
    first = own_w.shape[0]
    at = first + own_r.shape[0]
    for d in range(NY):
        total_r = own_r[d * recv : (d + 1) * recv, :] + got[first + d * recv : first + (d + 1) * recv, :].astype(F32)
        if d == 0:
            keep_r[...] = total_r
        else:
            staged[d - 1] = total_r.astype(BF16)
    copy = pltpu.make_async_copy(staged, r_all, sem)
    copy.start()
    summed = split_rows(join_rows(own_small[...]) + join_rows(got[at : at + SMALL, :]))
    small[...] = summed
    for d in range(NY):
        total_w = own_w[d * rows : (d + 1) * rows, :] + got[d * rows : (d + 1) * rows, :].astype(F32)
        if d == 0:
            keep[...] = total_w
        else:
            ref = sends[d - 1]
            ref[0:rows, :] = total_w.astype(BF16)
            ref[rows : rows + SMALL, :] = summed
    copy.wait()


def add_smalls(smalls, own, gots, me, size):
    smalls[me] = own
    for d, got in enumerate(gots):
        smalls[lax.rem(me + size - 1 - d, size)] = got
    total = join_rows(smalls[0])
    for i in range(1, size):
        total = total + join_rows(smalls[i])
    return split_rows(total)


def first_body(place, keep, small, got1, got2, got3, keep_2, small_2, send1, send2, send3, total, smalls):
    me, next_me = place[0], place[1]
    n = keep.shape[0]
    summed = keep[...]
    for got in (got1, got2, got3):
        summed = summed + got[0:n, :].astype(F32)
    total[...] = summed
    small_2[...] = add_smalls(smalls, small[...], [got[n : n + SMALL, :] for got in (got1, got2, got3)], me, NY)
    part = n // NX
    keep_2[...] = total[pl.ds(pl.multiple_of(next_me * part, part), part), :]
    for d, ref in ((1, send1), (2, send2), (3, send3)):
        at = pl.multiple_of(((next_me + d) & (NX - 1)) * part, part)
        ref[0:part, :] = total[pl.ds(at, part), :].astype(BF16)
        ref[part : part + SMALL, :] = small_2[...]


def second_body(
    place, keep, small, got1, got2, got3, up, got_up, down, got_down, r_all, out, out_up, out_down, r1, smalls, sem
):
    copy = pltpu.make_async_copy(r_all.at[0], r1, sem)
    copy.start()
    gots = (got1, got2, got3)
    n = keep.shape[0]
    summed = keep[...]
    for got in gots:
        summed = summed + got[0:n, :].astype(F32)
    out[0:n, :] = summed.astype(BF16)
    out[n : n + SMALL, :] = add_smalls(smalls, small[...], [got[n : n + SMALL, :] for got in gots], place[1], NX)
    add_pair([(up, got_up, out_up, 0), (down, got_down, out_down, 0)])
    copy.wait()


def merge(a, b, out):
    n = a.shape[0] - SMALL
    out[0:n, :] = (a[0:n, :].astype(F32) + b[0:n, :].astype(F32)).astype(BF16)
    out[n : n + SMALL, :] = split_rows(join_rows(a[n : n + SMALL, :]) + join_rows(b[n : n + SMALL, :]))


def merge_body(a, b, r_all, out, r2, sem):
    copy = pltpu.make_async_copy(r_all.at[1], r2, sem)
    copy.start()
    merge(a, b, out)
    copy.wait()


def merge_recv_body(a, b, r_all, keep_r, got_r1, out, r3, total_r, sem):
    copy = pltpu.make_async_copy(r_all.at[2], r3, sem)
    copy.start()
    merge(a, b, out)
    total_r[...] = keep_r[...] + got_r1[...].astype(F32)
    copy.wait()


def last_merge_body(a, b, keep_r, got_r2, got_r3, up, got_up, down, got_down, out, small, total_r, out_up, out_down):
    n = a.shape[0] - SMALL
    out[...] = (a[0:n, :].astype(F32) + b[0:n, :].astype(F32)).astype(BF16)
    small[...] = split_rows(join_rows(a[n : n + SMALL, :]) + join_rows(b[n : n + SMALL, :]))
    total_r[...] = keep_r[...] + got_r2[...].astype(F32) + got_r3[...].astype(F32)
    add_pair([(up, got_up, out_up, 0), (down, got_down, out_down, 0)])


def lay_part_body(place, own, got1, got2, got3, mine, up, down, out, keep, *sends):
    n = own.shape[0]
    for d, ref in enumerate((own, got1, got2, got3)):
        at = pl.multiple_of(((place[1] + d) & (NX - 1)) * n, n)
        out[pl.ds(at, n), :] = ref[...]
    turn(mine, up, down, keep, sends)


def stack_weights_body(own, got1, got2, got3, small, keep, send1, send2, send3, recv, w1, out, grad_nodes):
    n = own.shape[0]
    for d, ref in enumerate((own, got1, got2, got3)):
        out[d * n : (d + 1) * n, :] = ref[...]
    out[NY * n :, :] = small[...]
    nodes(keep, send1, send2, send3, recv, w1, grad_nodes)


def lay_half_body(place, pieces, *refs):
    laid, sems = refs[-2:]
    n, half = laid.shape[1:]
    if len(refs) > 4:
        mine, (grad_w1, grad_w2, *smalls) = refs[2], refs[3:8]
        other = join_rows(pieces[NY * n : NY * n + SMALL, :])
        small = jnp.where(place[1] == 0, other, join_rows(mine[...]))
        for i, ref in enumerate(smalls):
            for h in range(2):
                ref[:, h * half : (h + 1) * half] = small[2 * i + h : 2 * i + h + 1, :]
    else:
        grad_w1, grad_w2 = refs[:2]
    cols = pl.ds(pl.multiple_of(place[1] * half, half), half)
    for d in range(NY):
        i = (place[0] + d) & (NY - 1)
        laid[d] = pieces[d * n : (d + 1) * n, :].astype(F32)

        @pl.when(i < NY - 1)
        def _():
            rows = pl.ds(pl.multiple_of(i * n, n), n)
            pltpu.make_async_copy(laid.at[d], grad_w1.at[rows, cols], sems.at[d]).start()

        @pl.when(i == NY - 1)
        def _():
            pltpu.make_async_copy(laid.at[d], grad_w2.at[:, cols], sems.at[d]).start()

    for d in range(NY):
        pltpu.make_async_copy(laid.at[d], grad_w2.at[:, pl.ds(0, half)], sems.at[d]).wait()


def lay_half(place, pieces, rows, so_far=()):
    half = pieces.shape[1]
    vmem = pl.BlockSpec(memory_space=pltpu.VMEM)
    hbm = pl.BlockSpec(memory_space=pl.ANY)
    out_shape = [shaped((NY - 1) * rows, 2 * half, dtype=F32), shaped(rows, 2 * half, dtype=F32)]
    out_shape += [shaped(1, 2 * half, dtype=F32)] * 3 if so_far else []
    return call(
        lay_half_body,
        out_shape,
        [pieces, *so_far],
        "lay_half",
        scalars=[place],
        where=[vmem] + ([hbm, hbm, vmem] if so_far else []),
        to=[hbm, hbm] + ([vmem] * 3 if so_far else []),
        scratch=[pltpu.VMEM((NY, rows, half), F32), pltpu.SemaphoreType.DMA((NY,))],
        aliases={2: 0, 3: 1} if so_far else {},
    )


def z_ring(up, down):
    return push(up, "z", NZ, 1), push(down, "z", NZ, -1)


def flip(value, bit):
    return lax.ppermute(value, "z", [(i, i ^ bit) for i in range(NZ)])


def reduce_all(place, pay, own_w, own_r, own_small, pieces, w1):
    a0, a1, a2, a3, a4_lo, a4_hi, a5, a6, a7 = pieces
    share, width = a0.shape[1:]
    ring = [shaped(*a0.shape)] * 2
    half = pay.shape[1]
    rows, recv = own_w.shape[0] // NY, own_r.shape[0] // NY
    sum_r, part_r = shaped(recv, half, dtype=F32), shaped(recv, half)
    vmem = pl.BlockSpec(memory_space=pltpu.VMEM)
    hbm = pl.BlockSpec(memory_space=pl.ANY)
    dma = pltpu.SemaphoreType.DMA

    got = push(pay, "core", NCORE, 1)
    got_up, got_down = z_ring(a4_lo, a4_hi)
    out_shape = [shaped(rows, half, dtype=F32), shaped(SMALL, half), sum_r, shaped(3, recv, half)]
    keep, small, keep_r, r_all, *sends = call(
        core_body,
        out_shape + [shaped(rows + SMALL, half)] * 3,
        [own_w, own_r, own_small, got, a4_lo],
        "after_core",
        to=[vmem] * 3 + [hbm] + [vmem] * 3,
        scratch=[pltpu.VMEM((3, recv, half), BF16), dma],
    )
    gots = [swap(part, d + 1, True) for d, part in enumerate(sends)]
    up, down = call(first_add_body, ring, [a3, got_up, a5, got_down, small], "first_add")
    got_up, got_down = z_ring(up, down)

    part = rows // NX
    out_shape = [shaped(part, half, dtype=F32), shaped(SMALL, half)] + [shaped(part + SMALL, half)] * 3
    keep, small, *sends = call(
        first_body,
        out_shape,
        [keep, small, *gots],
        "after_first",
        scalars=[place],
        scratch=[pltpu.VMEM((rows, half), F32), pltpu.VMEM((NY, SMALL, half), BF16)],
    )
    gots = [swap(part, d + 1, False) for d, part in enumerate(sends)]
    payload = shaped(part + SMALL, half)
    value, up, down, r1 = call(
        second_body,
        [payload] + ring + [part_r],
        [keep, small, *gots, a2, got_up, a6, got_down, r_all],
        "after_second",
        scalars=[place],
        where=[vmem] * 9 + [hbm],
        scratch=[pltpu.VMEM((NX, SMALL, half), BF16), dma],
    )
    got_up, got_down = z_ring(up, down)
    got_r1 = push(r1, "y", NY, 1)
    value, r2 = call(
        merge_body, [payload, part_r], [value, flip(value, 1), r_all], "merge_1", where=[vmem] * 2 + [hbm], scratch=[dma]
    )
    got_r2 = push(r2, "y", NY, 2)
    value, r3, keep_r = call(
        merge_recv_body,
        [payload, part_r, sum_r],
        [value, flip(value, 2), r_all, keep_r, got_r1],
        "merge_2",
        where=[vmem] * 2 + [hbm] + [vmem] * 2,
        scratch=[dma],
    )
    got_r3 = push(r3, "y", NY, 3)
    value, small, recv_sum, up, down = call(
        last_merge_body,
        [shaped(part, half), shaped(SMALL, half), sum_r] + ring,
        [value, flip(value, 4), keep_r, got_r2, got_r3, a1, got_up, a7, got_down],
        "merge_4",
    )
    got_up, got_down = z_ring(up, down)
    gots = [swap(value, -d, False) for d in (1, 2, 3)]
    out_shape = [shaped(rows, half), shaped(share, width, dtype=F32)] + [shaped(share, width)] * 3
    value, keep, *sends = call(
        lay_part_body,
        out_shape,
        [value, *gots, a0, got_up, got_down],
        "lay_part",
        scalars=[place],
    )
    gots = [swap(value, -d, True) for d in (1, 2, 3)]
    send_sum = [keep] + [push(part, "x", NX, d + 1) for d, part in enumerate(sends)]
    mine, grad_nodes = call(
        stack_weights_body,
        [shaped(NY * rows + SMALL, half), shaped(share, width, dtype=F32)],
        [value, *gots, small, *send_sum, recv_sum, w1],
        "stack_weights",
        flops=100_000_000,
    )
    other = push(mine, "core", NCORE, 1)
    core = place[2]
    laid = lay_half(jnp.stack([place[0], core]), mine, rows)
    grad_w1, grad_w2, *small = lay_half(jnp.stack([place[1], 1 - core]), other, rows, [*laid, mine[NY * rows :]])
    return grad_w1, grad_w2, [s.reshape(-1) for s in small], grad_nodes


def nodes(keep, got1, got2, got3, recv, w1, out):
    share, width = keep.shape
    half = recv.shape[1]
    total = keep[...] + got1[...].astype(F32) + got2[...].astype(F32) + got3[...].astype(F32)
    total_r = recv[...].astype(BF16)
    out[...] = (
        mm(total.astype(BF16), w1[width : 2 * width, :], ((1,), (1,)))
        + mm(total_r[0:share, :], w1[2 * width :, 0:half], ((1,), (1,)))
        + mm(total_r[share:, :], w1[2 * width :, half:], ((1,), (1,)))
    )


def local(node_latents, edge_latents, cotangent, senders, receivers, edge_count, w1, b1, w2, b2, gamma):
    slots, width = edge_latents.shape[2:]
    share = node_latents.shape[0]
    edges = edge_latents.reshape(slots, width)
    cots = cotangent.reshape(slots, width)
    x, z, y, core = [lax.axis_index(name).astype(jnp.int32) for name in ("x", "z", "y", "core")]
    scalars = jnp.stack([edge_count.reshape(()), core, y, x, z])
    place = jnp.stack([jnp.where(core == 0, y, x), jnp.where(core == 0, x, y), core])

    pieces_s, pieces_r = gather(node_latents)
    grad_edges, preb, pay, own_w, own_r, own_small = edge_kernel(
        scalars, senders, receivers, edges, cots, w1, w2, b1, b2, gamma, pieces_s, pieces_r
    )
    sums = scatter_kernel(scalars, senders, preb, share)
    grad_w1, grad_w2, small, grad_nodes = reduce_all(place, pay, own_w, own_r, own_small, sums, w1)
    return (
        grad_edges.reshape(1, 1, slots, width),
        grad_nodes,
        grad_w1,
        small[0],
        grad_w2,
        small[1],
        small[2],
    )


def solution(mesh):
    mesh = Mesh(mesh.devices.reshape(NX, NZ, NY, NCORE), ("x", "z", "y", "core"))
    row, col = ("x", "z"), ("y", "core")
    in_specs = (
        P(col + row, None),
        P(row, col, None, None),
        P(row, col, None, None),
        P(row, col, None),
        P(row, col, None),
        P(row, col),
        P(),
        P(),
        P(),
        P(),
        P(),
    )
    out_specs = (P(row, col, None, None), P(col + row, None), P(), P(), P(), P(), P())
    return jax.shard_map(local, mesh=mesh, in_specs=in_specs, out_specs=out_specs, check_vma=False)
```

```python
import functools

import jax
import jax.numpy as jnp
from jax import lax
from jax.experimental import pallas as pl
from jax.experimental.pallas import tpu as pltpu
from jax.sharding import Mesh, PartitionSpec as P

EPS = 1e-05
NX, NZ, NY, NCORE = 4, 8, 4, 2
BF16 = jnp.bfloat16
F32 = jnp.float32


def shift(value, axis, size, step):
    return lax.ppermute(value, axis, [(i, (i - step) % size) for i in range(size)])


def push(value, axis, size, step):
    return lax.ppermute(value, axis, [(i, (i + step) % size) for i in range(size)])


def swap(value, step, first):
    pairs = []
    for x in range(NX):
        for y in range(NY):
            for core in range(NCORE):
                to = (x, (y + step) % NY) if (core == 0) == first else ((x + step) % NX, y)
                pairs.append(((x * NY + y) * NCORE + core, (to[0] * NY + to[1]) * NCORE + core))
    return lax.ppermute(value, ("x", "y", "core"), pairs)


def stack_body(own, got1, got2, got3, out, again):
    for d, ref in enumerate((own, got1, got2, got3)):
        out[d] = ref[...]
    again[...] = own[...]


def gather(own):
    gots = [shift(own, "x", NX, d) for d in (1, 2, 3)]
    along_x, own = call(stack_body, [shaped(NX, *own.shape), shaped(*own.shape)], [own, *gots], "stack_x")
    a = {0: along_x}
    for d in (1, 2, 3):
        a[d] = shift(a[d - 1], "z", NZ, 1)
        a[NZ - d] = shift(a[(NZ - d + 1) % NZ], "z", NZ, -1)
    a4_lo = shift(a[3][:2], "z", NZ, 1)
    a4_hi = shift(a[5][2:], "z", NZ, -1)
    along_y = jnp.stack([own] + [shift(own, "y", NY, d) for d in (1, 2, 3)])
    pieces_s = [a[0], a[1], a[2], a[3], a4_lo, a4_hi, a[5], a[6], a[7]]
    return pieces_s, [along_y, shift(along_y, "core", NCORE, 1)]


PLACES = [(0, 0, 4), (1, 0, 4), (2, 0, 4), (3, 0, 4), (4, 0, 2), (4, 2, 2), (5, 0, 4), (6, 0, 4), (7, 0, 4)]
SMALL = 16


def mm(a, b, dims):
    return lax.dot_general(a, b, ((dims[0], dims[1]), ((), ())), preferred_element_type=F32)


def one_hot(hit):
    return jnp.where(hit, 1.0, 0.0).astype(BF16)


def split_rows(values):
    high = values.astype(BF16).astype(F32)
    return jnp.concatenate([high, values - high, jnp.zeros((4, values.shape[1]), F32)], axis=0).astype(BF16)


def join_rows(rows):
    rows = rows.astype(F32)
    return rows[0:6] + rows[6:12]


def call(body, out_shape, args, name, scalars=(), scratch=(), flops=1_000_000, where=None, to=None, aliases=None, limit=24):
    vmem = pl.BlockSpec(memory_space=pltpu.VMEM)
    bytes_accessed = sum(a.size * a.dtype.itemsize for a in list(args) + list(out_shape))
    return pl.pallas_call(
        body,
        out_shape=out_shape,
        in_specs=[pl.BlockSpec(memory_space=pltpu.SMEM)] * len(scalars) + (where or [vmem] * len(args)),
        out_specs=to or [vmem] * len(out_shape),
        scratch_shapes=list(scratch),
        input_output_aliases=aliases or {},
        compiler_params=pltpu.CompilerParams(vmem_limit_bytes=limit * 2**20),
        cost_estimate=pl.CostEstimate(flops=flops, bytes_accessed=bytes_accessed, transcendentals=0),
        name=name,
    )(*scalars, *args)


def shaped(*shape, dtype=BF16):
    return jax.ShapeDtypeStruct(shape, dtype)


def owner_of(ids, share):
    scale = (1 << 22) // share + 1
    owner = jnp.right_shift(ids * scale, 22)
    return owner, ids - owner * share


def send_place(ids, scalars, share):
    owner, rest = owner_of(ids, share)
    dz = (owner - scalars[4]) & (NZ - 1)
    dx = (jnp.right_shift(owner, 3) - scalars[3]) & (NX - 1)
    return (dz * NX + dx) * share + rest


def recv_place(ids, scalars, share):
    owner, rest = owner_of(ids, share)
    dcore = (owner - scalars[1]) & (NCORE - 1)
    dy = (jnp.right_shift(owner, 1) - scalars[2]) & (NY - 1)
    return (dcore * NY + dy) * share + rest


def columns(ids, out):
    turned = jnp.transpose(ids)
    lanes = ids.shape[1]
    for j in range(ids.shape[0]):
        out[j * lanes : (j + 1) * lanes, :] = turned[:, j : j + 1]


def edge_kernel_body(tile, scalars, *refs):
    send_ids, recv_ids, recv_row, b1, b2, gamma = refs[:6]
    edges_hbm, cots_hbm, w1_hbm, w2_hbm = refs[6:10]
    pieces_s, pieces_r = refs[10:19], refs[19:21]
    grad_edges_hbm, preb_hbm, pay_hbm, own_w, own_r, own_small = refs[21:27]
    lat_s, lat_r, lefts, cots, w1, w2, rights, grad_edges, pay, sid_col, rid_col, sems, out_sems = refs[27:]
    count, core, x, y = scalars[0], scalars[1], scalars[3], scalars[2]
    slots, width = cots.shape
    half = width // 2
    share = lat_s.shape[2]
    nodes = NZ * NX * share
    block = NCORE * NY * share
    edges, x_s, x_r, activ = [lefts.at[i] for i in range(4)]
    preb, goutb = rights.at[0], rights.at[1]
    started = []

    def send_out(src, dst):
        copy = pltpu.make_async_copy(src, dst, out_sems.at[len(started)])
        copy.start()
        started.append(copy)

    copies = [(ref, lat_r.at[pl.ds(i * NY, NY)]) for i, ref in enumerate(pieces_r)]
    copies += [(ref, lat_s.at[dz, pl.ds(dx, n)]) for ref, (dz, dx, n) in zip(pieces_s, PLACES)]
    copies += [(w1_hbm, w1), (edges_hbm, edges), (w2_hbm, w2), (cots_hbm, cots)]
    copies = [pltpu.make_async_copy(src, dst, sems.at[i]) for i, (src, dst) in enumerate(copies)]
    for copy in copies:
        copy.start()
    columns(send_place(send_ids[...], scalars, share), sid_col)
    columns(recv_place(recv_ids[...], scalars, share), rid_col)
    zero = jnp.zeros((1, width), F32)
    sum_b1, sum_b2, sum_gain = zero, zero, zero
    for t in range(slots // tile):
        rows = slice(t * tile, (t + 1) * tile)
        hot_r = one_hot(rid_col[rows, :] == lax.broadcasted_iota(jnp.int32, (tile, block), 1))
        hot_s = one_hot(sid_col[rows, :] == lax.broadcasted_iota(jnp.int32, (tile, nodes), 1))
        if t == 0:
            for copy in copies[:11]:
                copy.wait()
        xr = mm(hot_r, lat_r[...].reshape(block, width), ((1,), (0,))).astype(BF16)
        xs = mm(hot_s, lat_s[...].reshape(nodes, width), ((1,), (0,))).astype(BF16)
        x_s[rows, :] = xs
        x_r[rows, :] = xr
        if t == 0:
            for copy in copies[11:13]:
                copy.wait()
        pre = (
            mm(xr, w1[2 * width :, :], ((1,), (0,)))
            + mm(xs, w1[width : 2 * width, :], ((1,), (0,)))
            + mm(edges[rows, :], w1[0:width, :], ((1,), (0,)))
            + b1[...]
        )
        sigma = jax.nn.sigmoid(pre)
        act = (pre * sigma).astype(BF16)
        slope = sigma * (1.0 + pre * (1.0 - sigma))
        activ[rows, :] = act
        if t == 0:
            for copy in copies[13:]:
                copy.wait()
        output = mm(act, w2[...], ((1,), (0,))) + b2[...]
        centred = output - jnp.mean(output, axis=1, keepdims=True)
        inv_std = lax.rsqrt(jnp.mean(centred * centred, axis=1, keepdims=True) + EPS)
        normed = centred * inv_std
        live = t * tile + lax.broadcasted_iota(jnp.int32, (tile, 1), 0) < count
        g = jnp.where(live, cots[rows, :].astype(F32), 0.0)
        sum_gain = sum_gain + jnp.sum(g * normed, axis=0, keepdims=True)
        grad_norm = g * gamma[...]
        grad_out = inv_std * (
            grad_norm
            - jnp.mean(grad_norm, axis=1, keepdims=True)
            - normed * jnp.mean(grad_norm * normed, axis=1, keepdims=True)
        )
        gob = grad_out.astype(BF16)
        goutb[rows, :] = gob
        sum_b2 = sum_b2 + jnp.sum(grad_out, axis=0, keepdims=True)
        grad_pre = mm(gob, w2[...], ((1,), (1,))) * slope
        sum_b1 = sum_b1 + jnp.sum(grad_pre, axis=0, keepdims=True)
        gpb = grad_pre.astype(BF16)
        preb[rows, :] = gpb
        grad_edges[rows, :] = (g + mm(gpb, w1[0:width, :], ((1,), (1,)))).astype(BF16)
    send_out(preb, preb_hbm)
    send_out(grad_edges, grad_edges_hbm)

    first = NY * width
    rid_row = recv_place(recv_row[...], scalars, share)
    for core_at in range(NCORE):
        ids = core_at * NY * share + lax.broadcasted_iota(jnp.int32, (NY * share, slots), 0)
        sums_r = mm(one_hot(rid_row == ids), preb[...], ((1,), (0,)))
        for d in range(NY):
            for h in range(2):
                part = sums_r[d * share : (d + 1) * share, h * half : (h + 1) * half]
                at = (2 * d + h) * share
                if core_at == 0:
                    own_r[at : at + share, :] = part
                else:
                    pay[first + at : first + at + share, :] = part.astype(BF16)
    parts = [s[:, h * half : (h + 1) * half] for s in (sum_b1, sum_b2, sum_gain) for h in range(2)]
    small = split_rows(jnp.concatenate(parts, axis=0))
    own_small[...] = small
    at = first + 2 * NY * share
    pay[at : at + SMALL, :] = small
    send_out(pay.at[pl.ds(first, at + SMALL - first)], pay_hbm.at[pl.ds(first, at + SMALL - first)])

    own = pl.ds(pl.multiple_of(core * half, half), half)
    peer = pl.ds(pl.multiple_of((1 - core) * half, half), half)
    mine = jnp.where(core == 0, y, x)
    others = jnp.where(core == 0, x, y)
    for cols, axis_at, ref, hbm in ((peer, others, pay, pay_hbm), (own, mine, own_w, None)):
        for d in range(NY):
            i = (axis_at + d) & (NY - 1)
            right = jnp.where(i == NY - 1, 1, 0)
            rows = pl.ds(d * width, width)
            ref[rows, :] = mm(lefts[i], rights[right, :, cols], ((0,), (0,))).astype(ref.dtype)
            if hbm is not None:
                send_out(ref.at[rows], hbm.at[rows])
    for copy in started:
        copy.wait()


def edge_kernel(scalars, senders, receivers, edges, cots, w1, w2, b1, b2, gamma, pieces_s, pieces_r):
    slots, width = edges.shape
    half = width // 2
    share = pieces_s[0].shape[1]
    vmem = pl.BlockSpec(memory_space=pltpu.VMEM)
    hbm = pl.BlockSpec(memory_space=pl.ANY)
    recv_rows = 2 * NY * share
    out_shape = [
        shaped(slots, width),
        shaped(slots, width),
        shaped(NY * width + recv_rows + SMALL, half),
        shaped(NY * width, half, dtype=F32),
        shaped(recv_rows, half, dtype=F32),
        shaped(SMALL, half),
    ]
    return call(
        functools.partial(edge_kernel_body, 1024),
        out_shape,
        [
            senders.reshape(-1, 128),
            receivers.reshape(-1, 128),
            receivers.reshape(1, slots),
            b1.reshape(1, width),
            b2.reshape(1, width),
            gamma.reshape(1, width),
            edges,
            cots,
            w1,
            w2,
            *pieces_s,
            *pieces_r,
        ],
        "edge_step",
        scalars=[scalars],
        where=[vmem] * 6 + [hbm] * 15,
        to=[hbm] * 3 + [vmem] * 3,
        scratch=[
            pltpu.VMEM((NZ, NX, share, width), BF16),
            pltpu.VMEM((NCORE * NY, share, width), BF16),
            pltpu.VMEM((4, slots, width), BF16),
            pltpu.VMEM((slots, width), BF16),
            pltpu.VMEM(w1.shape, BF16),
            pltpu.VMEM(w2.shape, BF16),
            pltpu.VMEM((2, slots, width), BF16),
            pltpu.VMEM((slots, width), BF16),
            pltpu.VMEM(out_shape[2].shape, BF16),
            pltpu.VMEM((slots, 1), jnp.int32),
            pltpu.VMEM((slots, 1), jnp.int32),
            pltpu.SemaphoreType.DMA((15,)),
            pltpu.SemaphoreType.DMA((12,)),
        ],
        flops=10_000_000_000,
        limit=56,
    )


def scatter_body(scalars, send_row, preb, *outs):
    slots, width = preb.shape
    share = outs[0].shape[1]
    grads = preb[...]
    sid_row = send_place(send_row[...], scalars, share)
    for dz, ref in enumerate(outs):
        hit = sid_row == dz * NX * share + lax.broadcasted_iota(jnp.int32, (NX * share, slots), 0)
        ref[...] = mm(one_hot(hit), grads, ((1,), (0,))).astype(BF16).reshape(NX, share, width)


def scatter_kernel(scalars, senders, preb, share):
    slots, width = preb.shape
    out_shape = [shaped(NX, share, width)] * NZ
    args = [senders.reshape(1, slots), preb]
    return call(scatter_body, out_shape, args, "scatter", scalars=[scalars], flops=3_000_000_000, limit=48)


def add_pair(pairs):
    for mine, got, out, first in pairs:
        n, size = got.shape[0], mine.shape[0]
        out[first : first + n] = (mine[first : first + n].astype(F32) + got[...].astype(F32)).astype(BF16)
        if first > 0:
            out[0:first] = mine[0:first]
        if first + n < size:
            out[first + n : size] = mine[first + n : size]


def first_add_body(up, got_up, down, after, out_up, out_down):
    add_pair([(up, got_up, out_up, 0)])
    out_down[...] = down[...]


def turn(mine, up, down, keep, sends):
    total = mine[...].astype(F32) + up[...].astype(F32) + down[...].astype(F32)
    keep[...] = total[0]
    for d, ref in enumerate(sends):
        ref[...] = total[d + 1].astype(BF16)


def core_body(own_w, own_r, own_small, got, after, keep, small, keep_r, r_all, *refs):
    sends, (staged, sem) = refs[:3], refs[3:]
    rows, recv = own_w.shape[0] // NY, own_r.shape[0] // NY
    first = own_w.shape[0]
    at = first + own_r.shape[0]
    for d in range(NY):
        total_r = own_r[d * recv : (d + 1) * recv, :] + got[first + d * recv : first + (d + 1) * recv, :].astype(F32)
        if d == 0:
            keep_r[...] = total_r
        else:
            staged[d - 1] = total_r.astype(BF16)
    copy = pltpu.make_async_copy(staged, r_all, sem)
    copy.start()
    summed = split_rows(join_rows(own_small[...]) + join_rows(got[at : at + SMALL, :]))
    small[...] = summed
    for d in range(NY):
        total_w = own_w[d * rows : (d + 1) * rows, :] + got[d * rows : (d + 1) * rows, :].astype(F32)
        if d == 0:
            keep[...] = total_w
        else:
            ref = sends[d - 1]
            ref[0:rows, :] = total_w.astype(BF16)
            ref[rows : rows + SMALL, :] = summed
    copy.wait()


def add_smalls(smalls, own, gots, me, size):
    smalls[me] = own
    for d, got in enumerate(gots):
        smalls[lax.rem(me + size - 1 - d, size)] = got
    total = join_rows(smalls[0])
    for i in range(1, size):
        total = total + join_rows(smalls[i])
    return split_rows(total)


def first_body(place, keep, small, got1, got2, got3, keep_2, small_2, send1, send2, send3, total, smalls):
    me, next_me = place[0], place[1]
    n = keep.shape[0]
    summed = keep[...]
    for got in (got1, got2, got3):
        summed = summed + got[0:n, :].astype(F32)
    total[...] = summed
    small_2[...] = add_smalls(smalls, small[...], [got[n : n + SMALL, :] for got in (got1, got2, got3)], me, NY)
    part = n // NX
    keep_2[...] = total[pl.ds(pl.multiple_of(next_me * part, part), part), :]
    for d, ref in ((1, send1), (2, send2), (3, send3)):
        at = pl.multiple_of(((next_me + d) & (NX - 1)) * part, part)
        ref[0:part, :] = total[pl.ds(at, part), :].astype(BF16)
        ref[part : part + SMALL, :] = small_2[...]


def second_body(
    place, keep, small, got1, got2, got3, up, got_up, down, got_down, r_all, out, out_up, out_down, r1, smalls, sem
):
    copy = pltpu.make_async_copy(r_all.at[0], r1, sem)
    copy.start()
    gots = (got1, got2, got3)
    n = keep.shape[0]
    summed = keep[...]
    for got in gots:
        summed = summed + got[0:n, :].astype(F32)
    out[0:n, :] = summed.astype(BF16)
    out[n : n + SMALL, :] = add_smalls(smalls, small[...], [got[n : n + SMALL, :] for got in gots], place[1], NX)
    add_pair([(up, got_up, out_up, 0), (down, got_down, out_down, 0)])
    copy.wait()


def merge(a, b, out):
    n = a.shape[0] - SMALL
    out[0:n, :] = (a[0:n, :].astype(F32) + b[0:n, :].astype(F32)).astype(BF16)
    out[n : n + SMALL, :] = split_rows(join_rows(a[n : n + SMALL, :]) + join_rows(b[n : n + SMALL, :]))


def merge_body(a, b, r_all, out, r2, sem):
    copy = pltpu.make_async_copy(r_all.at[1], r2, sem)
    copy.start()
    merge(a, b, out)
    copy.wait()


def merge_recv_body(a, b, r_all, keep_r, got_r1, out, r3, total_r, sem):
    copy = pltpu.make_async_copy(r_all.at[2], r3, sem)
    copy.start()
    merge(a, b, out)
    total_r[...] = keep_r[...] + got_r1[...].astype(F32)
    copy.wait()


def last_merge_body(a, b, keep_r, got_r2, got_r3, up, got_up, down, got_down, out, small, total_r, out_up, out_down):
    n = a.shape[0] - SMALL
    out[...] = (a[0:n, :].astype(F32) + b[0:n, :].astype(F32)).astype(BF16)
    small[...] = split_rows(join_rows(a[n : n + SMALL, :]) + join_rows(b[n : n + SMALL, :]))
    total_r[...] = keep_r[...] + got_r2[...].astype(F32) + got_r3[...].astype(F32)
    add_pair([(up, got_up, out_up, 0), (down, got_down, out_down, 0)])


def lay_part_body(place, own, got1, got2, got3, mine, up, down, out, keep, *sends):
    n = own.shape[0]
    for d, ref in enumerate((own, got1, got2, got3)):
        at = pl.multiple_of(((place[1] + d) & (NX - 1)) * n, n)
        out[pl.ds(at, n), :] = ref[...]
    turn(mine, up, down, keep, sends)


def stack_weights_body(own, got1, got2, got3, small, keep, send1, send2, send3, recv, w1, out, grad_nodes):
    n = own.shape[0]
    for d, ref in enumerate((own, got1, got2, got3)):
        out[d * n : (d + 1) * n, :] = ref[...]
    out[NY * n :, :] = small[...]
    nodes(keep, send1, send2, send3, recv, w1, grad_nodes)


def lay_half_body(place, pieces, *refs):
    laid, sems = refs[-2:]
    n, half = laid.shape[1:]
    if len(refs) > 4:
        mine, (grad_w1, grad_w2, *smalls) = refs[2], refs[3:8]
        other = join_rows(pieces[NY * n : NY * n + SMALL, :])
        small = jnp.where(place[1] == 0, other, join_rows(mine[...]))
        for i, ref in enumerate(smalls):
            for h in range(2):
                ref[:, h * half : (h + 1) * half] = small[2 * i + h : 2 * i + h + 1, :]
    else:
        grad_w1, grad_w2 = refs[:2]
    cols = pl.ds(pl.multiple_of(place[1] * half, half), half)
    for d in range(NY):
        i = (place[0] + d) & (NY - 1)
        laid[d] = pieces[d * n : (d + 1) * n, :].astype(F32)

        @pl.when(i < NY - 1)
        def _():
            rows = pl.ds(pl.multiple_of(i * n, n), n)
            pltpu.make_async_copy(laid.at[d], grad_w1.at[rows, cols], sems.at[d]).start()

        @pl.when(i == NY - 1)
        def _():
            pltpu.make_async_copy(laid.at[d], grad_w2.at[:, cols], sems.at[d]).start()

    for d in range(NY):
        pltpu.make_async_copy(laid.at[d], grad_w2.at[:, pl.ds(0, half)], sems.at[d]).wait()


def lay_half(place, pieces, rows, so_far=()):
    half = pieces.shape[1]
    vmem = pl.BlockSpec(memory_space=pltpu.VMEM)
    hbm = pl.BlockSpec(memory_space=pl.ANY)
    out_shape = [shaped((NY - 1) * rows, 2 * half, dtype=F32), shaped(rows, 2 * half, dtype=F32)]
    out_shape += [shaped(1, 2 * half, dtype=F32)] * 3 if so_far else []
    return call(
        lay_half_body,
        out_shape,
        [pieces, *so_far],
        "lay_half",
        scalars=[place],
        where=[vmem] + ([hbm, hbm, vmem] if so_far else []),
        to=[hbm, hbm] + ([vmem] * 3 if so_far else []),
        scratch=[pltpu.VMEM((NY, rows, half), F32), pltpu.SemaphoreType.DMA((NY,))],
        aliases={2: 0, 3: 1} if so_far else {},
    )


def z_ring(up, down):
    return push(up, "z", NZ, 1), push(down, "z", NZ, -1)


def flip(value, bit):
    return lax.ppermute(value, "z", [(i, i ^ bit) for i in range(NZ)])


def reduce_all(place, pay, own_w, own_r, own_small, pieces, w1):
    a0, a1, a2, a3, a4, a5, a6, a7 = pieces
    share, width = a0.shape[1:]
    ring = [shaped(*a0.shape)] * 2
    half = pay.shape[1]
    rows, recv = own_w.shape[0] // NY, own_r.shape[0] // NY
    sum_r, part_r = shaped(recv, half, dtype=F32), shaped(recv, half)
    vmem = pl.BlockSpec(memory_space=pltpu.VMEM)
    hbm = pl.BlockSpec(memory_space=pl.ANY)
    dma = pltpu.SemaphoreType.DMA

    got = push(pay, "core", NCORE, 1)
    got_up = push(a4, "z", NZ, 1)
    out_shape = [shaped(rows, half, dtype=F32), shaped(SMALL, half), sum_r, shaped(3, recv, half)]
    keep, small, keep_r, r_all, *sends = call(
        core_body,
        out_shape + [shaped(rows + SMALL, half)] * 3,
        [own_w, own_r, own_small, got, a4],
        "after_core",
        to=[vmem] * 3 + [hbm] + [vmem] * 3,
        scratch=[pltpu.VMEM((3, recv, half), BF16), dma],
    )
    gots = [swap(part, d + 1, True) for d, part in enumerate(sends)]
    up, down = call(first_add_body, ring, [a3, got_up, a5, small], "first_add")
    got_up, got_down = z_ring(up, down)

    part = rows // NX
    out_shape = [shaped(part, half, dtype=F32), shaped(SMALL, half)] + [shaped(part + SMALL, half)] * 3
    keep, small, *sends = call(
        first_body,
        out_shape,
        [keep, small, *gots],
        "after_first",
        scalars=[place],
        scratch=[pltpu.VMEM((rows, half), F32), pltpu.VMEM((NY, SMALL, half), BF16)],
    )
    gots = [swap(part, d + 1, False) for d, part in enumerate(sends)]
    payload = shaped(part + SMALL, half)
    value, up, down, r1 = call(
        second_body,
        [payload] + ring + [part_r],
        [keep, small, *gots, a2, got_up, a6, got_down, r_all],
        "after_second",
        scalars=[place],
        where=[vmem] * 9 + [hbm],
        scratch=[pltpu.VMEM((NX, SMALL, half), BF16), dma],
    )
    got_up, got_down = z_ring(up, down)
    got_r1 = push(r1, "y", NY, 1)
    value, r2 = call(
        merge_body, [payload, part_r], [value, flip(value, 1), r_all], "merge_1", where=[vmem] * 2 + [hbm], scratch=[dma]
    )
    got_r2 = push(r2, "y", NY, 2)
    value, r3, keep_r = call(
        merge_recv_body,
        [payload, part_r, sum_r],
        [value, flip(value, 2), r_all, keep_r, got_r1],
        "merge_2",
        where=[vmem] * 2 + [hbm] + [vmem] * 2,
        scratch=[dma],
    )
    got_r3 = push(r3, "y", NY, 3)
    value, small, recv_sum, up, down = call(
        last_merge_body,
        [shaped(part, half), shaped(SMALL, half), sum_r] + ring,
        [value, flip(value, 4), keep_r, got_r2, got_r3, a1, got_up, a7, got_down],
        "merge_4",
    )
    got_up, got_down = z_ring(up, down)
    gots = [swap(value, -d, False) for d in (1, 2, 3)]
    out_shape = [shaped(rows, half), shaped(share, width, dtype=F32)] + [shaped(share, width)] * 3
    value, keep, *sends = call(
        lay_part_body,
        out_shape,
        [value, *gots, a0, got_up, got_down],
        "lay_part",
        scalars=[place],
    )
    gots = [swap(value, -d, True) for d in (1, 2, 3)]
    send_sum = [keep] + [push(part, "x", NX, d + 1) for d, part in enumerate(sends)]
    mine, grad_nodes = call(
        stack_weights_body,
        [shaped(NY * rows + SMALL, half), shaped(share, width, dtype=F32)],
        [value, *gots, small, *send_sum, recv_sum, w1],
        "stack_weights",
        flops=100_000_000,
    )
    other = push(mine, "core", NCORE, 1)
    core = place[2]
    laid = lay_half(jnp.stack([place[0], core]), mine, rows)
    grad_w1, grad_w2, *small = lay_half(jnp.stack([place[1], 1 - core]), other, rows, [*laid, mine[NY * rows :]])
    return grad_w1, grad_w2, [s.reshape(-1) for s in small], grad_nodes


def nodes(keep, got1, got2, got3, recv, w1, out):
    share, width = keep.shape
    half = recv.shape[1]
    total = keep[...] + got1[...].astype(F32) + got2[...].astype(F32) + got3[...].astype(F32)
    total_r = recv[...].astype(BF16)
    out[...] = (
        mm(total.astype(BF16), w1[width : 2 * width, :], ((1,), (1,)))
        + mm(total_r[0:share, :], w1[2 * width :, 0:half], ((1,), (1,)))
        + mm(total_r[share:, :], w1[2 * width :, half:], ((1,), (1,)))
    )


def local(node_latents, edge_latents, cotangent, senders, receivers, edge_count, w1, b1, w2, b2, gamma):
    slots, width = edge_latents.shape[2:]
    share = node_latents.shape[0]
    edges = edge_latents.reshape(slots, width)
    cots = cotangent.reshape(slots, width)
    x, z, y, core = [lax.axis_index(name).astype(jnp.int32) for name in ("x", "z", "y", "core")]
    scalars = jnp.stack([edge_count.reshape(()), core, y, x, z])
    place = jnp.stack([jnp.where(core == 0, y, x), jnp.where(core == 0, x, y), core])

    pieces_s, pieces_r = gather(node_latents)
    grad_edges, preb, pay, own_w, own_r, own_small = edge_kernel(
        scalars, senders, receivers, edges, cots, w1, w2, b1, b2, gamma, pieces_s, pieces_r
    )
    sums = scatter_kernel(scalars, senders, preb, share)
    grad_w1, grad_w2, small, grad_nodes = reduce_all(place, pay, own_w, own_r, own_small, sums, w1)
    return (
        grad_edges.reshape(1, 1, slots, width),
        grad_nodes,
        grad_w1,
        small[0],
        grad_w2,
        small[1],
        small[2],
    )


def solution(mesh):
    mesh = Mesh(mesh.devices.reshape(NX, NZ, NY, NCORE), ("x", "z", "y", "core"))
    row, col = ("x", "z"), ("y", "core")
    in_specs = (
        P(col + row, None),
        P(row, col, None, None),
        P(row, col, None, None),
        P(row, col, None),
        P(row, col, None),
        P(row, col),
        P(),
        P(),
        P(),
        P(),
        P(),
    )
    out_specs = (P(row, col, None, None), P(col + row, None), P(), P(), P(), P(), P())
    return jax.shard_map(local, mesh=mesh, in_specs=in_specs, out_specs=out_specs, check_vma=False)
```

```python
import functools

import jax
import jax.numpy as jnp
from jax import lax
from jax.experimental import pallas as pl
from jax.experimental.pallas import tpu as pltpu
from jax.sharding import Mesh, PartitionSpec as P

EPS = 1e-05
NX, NZ, NY, NCORE = 4, 8, 4, 2
BF16 = jnp.bfloat16
F32 = jnp.float32


def shift(value, axis, size, step):
    return lax.ppermute(value, axis, [(i, (i - step) % size) for i in range(size)])


def push(value, axis, size, step):
    return lax.ppermute(value, axis, [(i, (i + step) % size) for i in range(size)])


def swap(value, step, first):
    pairs = []
    for x in range(NX):
        for y in range(NY):
            for core in range(NCORE):
                to = (x, (y + step) % NY) if (core == 0) == first else ((x + step) % NX, y)
                pairs.append(((x * NY + y) * NCORE + core, (to[0] * NY + to[1]) * NCORE + core))
    return lax.ppermute(value, ("x", "y", "core"), pairs)


def stack_body(own, got1, got2, got3, out, again):
    for d, ref in enumerate((own, got1, got2, got3)):
        out[d] = ref[...]
    again[...] = own[...]


def gather(own):
    gots = [shift(own, "x", NX, d) for d in (1, 2, 3)]
    along_x, own = call(stack_body, [shaped(NX, *own.shape), shaped(*own.shape)], [own, *gots], "stack_x")
    a = {0: along_x}
    for d in (1, 2, 3):
        a[d] = shift(a[d - 1], "z", NZ, 1)
        a[NZ - d] = shift(a[(NZ - d + 1) % NZ], "z", NZ, -1)
    a4_lo = shift(a[3][:2], "z", NZ, 1)
    a4_hi = shift(a[5][2:], "z", NZ, -1)
    along_y = jnp.stack([own] + [shift(own, "y", NY, d) for d in (1, 2, 3)])
    pieces_s = [a[0], a[1], a[2], a[3], a4_lo, a4_hi, a[5], a[6], a[7]]
    return pieces_s, [along_y, shift(along_y, "core", NCORE, 1)]


PLACES = [(0, 0, 4), (1, 0, 4), (2, 0, 4), (3, 0, 4), (4, 0, 2), (4, 2, 2), (5, 0, 4), (6, 0, 4), (7, 0, 4)]
SMALL = 16


def mm(a, b, dims):
    return lax.dot_general(a, b, ((dims[0], dims[1]), ((), ())), preferred_element_type=F32)


def one_hot(hit):
    return jnp.where(hit, 1.0, 0.0).astype(BF16)


def split_rows(values):
    high = values.astype(BF16).astype(F32)
    return jnp.concatenate([high, values - high, jnp.zeros((4, values.shape[1]), F32)], axis=0).astype(BF16)


def join_rows(rows):
    rows = rows.astype(F32)
    return rows[0:6] + rows[6:12]


def call(body, out_shape, args, name, scalars=(), scratch=(), flops=1_000_000, where=None, to=None, aliases=None, limit=24):
    vmem = pl.BlockSpec(memory_space=pltpu.VMEM)
    bytes_accessed = sum(a.size * a.dtype.itemsize for a in list(args) + list(out_shape))
    return pl.pallas_call(
        body,
        out_shape=out_shape,
        in_specs=[pl.BlockSpec(memory_space=pltpu.SMEM)] * len(scalars) + (where or [vmem] * len(args)),
        out_specs=to or [vmem] * len(out_shape),
        scratch_shapes=list(scratch),
        input_output_aliases=aliases or {},
        compiler_params=pltpu.CompilerParams(vmem_limit_bytes=limit * 2**20),
        cost_estimate=pl.CostEstimate(flops=flops, bytes_accessed=bytes_accessed, transcendentals=0),
        name=name,
    )(*scalars, *args)


def shaped(*shape, dtype=BF16):
    return jax.ShapeDtypeStruct(shape, dtype)


def owner_of(ids, share):
    scale = (1 << 22) // share + 1
    owner = jnp.right_shift(ids * scale, 22)
    return owner, ids - owner * share


def send_place(ids, scalars, share):
    owner, rest = owner_of(ids, share)
    dz = (owner - scalars[4]) & (NZ - 1)
    dx = (jnp.right_shift(owner, 3) - scalars[3]) & (NX - 1)
    return (dz * NX + dx) * share + rest


def recv_place(ids, scalars, share):
    owner, rest = owner_of(ids, share)
    dcore = (owner - scalars[1]) & (NCORE - 1)
    dy = (jnp.right_shift(owner, 1) - scalars[2]) & (NY - 1)
    return (dcore * NY + dy) * share + rest


def columns(ids, out):
    turned = jnp.transpose(ids)
    lanes = ids.shape[1]
    for j in range(ids.shape[0]):
        out[j * lanes : (j + 1) * lanes, :] = turned[:, j : j + 1]


def edge_kernel_body(tile, scalars, *refs):
    send_ids, recv_ids, recv_row, b1, b2, gamma = refs[:6]
    edges_hbm, cots_hbm, w1_hbm, w2_hbm = refs[6:10]
    pieces_s, pieces_r = refs[10:19], refs[19:21]
    grad_edges_hbm, preb_hbm, pay_hbm, own_w, own_r, own_small = refs[21:27]
    lat_s, lat_r, lefts, cots, w1, w2, rights, grad_edges, pay, sid_col, rid_col, sems, out_sems = refs[27:]
    count, core, x, y = scalars[0], scalars[1], scalars[3], scalars[2]
    slots, width = cots.shape
    half = width // 2
    share = lat_s.shape[2]
    nodes = NZ * NX * share
    block = NCORE * NY * share
    edges, x_s, x_r, activ = [lefts.at[i] for i in range(4)]
    preb, goutb = rights.at[0], rights.at[1]
    started = []

    def send_out(src, dst):
        copy = pltpu.make_async_copy(src, dst, out_sems.at[len(started)])
        copy.start()
        started.append(copy)

    copies = [(ref, lat_r.at[pl.ds(i * NY, NY)]) for i, ref in enumerate(pieces_r)]
    copies += [(ref, lat_s.at[dz, pl.ds(dx, n)]) for ref, (dz, dx, n) in zip(pieces_s, PLACES)]
    copies += [(w1_hbm, w1), (edges_hbm, edges), (w2_hbm, w2), (cots_hbm, cots)]
    copies = [pltpu.make_async_copy(src, dst, sems.at[i]) for i, (src, dst) in enumerate(copies)]
    for copy in copies:
        copy.start()
    columns(send_place(send_ids[...], scalars, share), sid_col)
    columns(recv_place(recv_ids[...], scalars, share), rid_col)
    zero = jnp.zeros((1, width), F32)
    sum_b1, sum_b2, sum_gain = zero, zero, zero
    for t in range(slots // tile):
        rows = slice(t * tile, (t + 1) * tile)
        hot_r = one_hot(rid_col[rows, :] == lax.broadcasted_iota(jnp.int32, (tile, block), 1))
        hot_s = one_hot(sid_col[rows, :] == lax.broadcasted_iota(jnp.int32, (tile, nodes), 1))
        if t == 0:
            for copy in copies[:11]:
                copy.wait()
        xr = mm(hot_r, lat_r[...].reshape(block, width), ((1,), (0,))).astype(BF16)
        xs = mm(hot_s, lat_s[...].reshape(nodes, width), ((1,), (0,))).astype(BF16)
        x_s[rows, :] = xs
        x_r[rows, :] = xr
        if t == 0:
            for copy in copies[11:13]:
                copy.wait()
        pre = (
            mm(xr, w1[2 * width :, :], ((1,), (0,)))
            + mm(xs, w1[width : 2 * width, :], ((1,), (0,)))
            + mm(edges[rows, :], w1[0:width, :], ((1,), (0,)))
            + b1[...]
        )
        sigma = jax.nn.sigmoid(pre)
        act = (pre * sigma).astype(BF16)
        slope = sigma * (1.0 + pre * (1.0 - sigma))
        activ[rows, :] = act
        if t == 0:
            for copy in copies[13:]:
                copy.wait()
        output = mm(act, w2[...], ((1,), (0,))) + b2[...]
        centred = output - jnp.mean(output, axis=1, keepdims=True)
        inv_std = lax.rsqrt(jnp.mean(centred * centred, axis=1, keepdims=True) + EPS)
        normed = centred * inv_std
        live = t * tile + lax.broadcasted_iota(jnp.int32, (tile, 1), 0) < count
        g = jnp.where(live, cots[rows, :].astype(F32), 0.0)
        sum_gain = sum_gain + jnp.sum(g * normed, axis=0, keepdims=True)
        grad_norm = g * gamma[...]
        grad_out = inv_std * (
            grad_norm
            - jnp.mean(grad_norm, axis=1, keepdims=True)
            - normed * jnp.mean(grad_norm * normed, axis=1, keepdims=True)
        )
        gob = grad_out.astype(BF16)
        goutb[rows, :] = gob
        sum_b2 = sum_b2 + jnp.sum(grad_out, axis=0, keepdims=True)
        grad_pre = mm(gob, w2[...], ((1,), (1,))) * slope
        sum_b1 = sum_b1 + jnp.sum(grad_pre, axis=0, keepdims=True)
        gpb = grad_pre.astype(BF16)
        preb[rows, :] = gpb
        grad_edges[rows, :] = (g + mm(gpb, w1[0:width, :], ((1,), (1,)))).astype(BF16)
    send_out(preb, preb_hbm)
    send_out(grad_edges, grad_edges_hbm)

    first = NY * width
    rid_row = recv_place(recv_row[...], scalars, share)
    for core_at in range(NCORE):
        ids = core_at * NY * share + lax.broadcasted_iota(jnp.int32, (NY * share, slots), 0)
        sums_r = mm(one_hot(rid_row == ids), preb[...], ((1,), (0,)))
        for d in range(NY):
            for h in range(2):
                part = sums_r[d * share : (d + 1) * share, h * half : (h + 1) * half]
                at = (2 * d + h) * share
                if core_at == 0:
                    own_r[at : at + share, :] = part
                else:
                    pay[first + at : first + at + share, :] = part.astype(BF16)
    parts = [s[:, h * half : (h + 1) * half] for s in (sum_b1, sum_b2, sum_gain) for h in range(2)]
    small = split_rows(jnp.concatenate(parts, axis=0))
    own_small[...] = small
    at = first + 2 * NY * share
    pay[at : at + SMALL, :] = small
    send_out(pay.at[pl.ds(first, at + SMALL - first)], pay_hbm.at[pl.ds(first, at + SMALL - first)])

    own = pl.ds(pl.multiple_of(core * half, half), half)
    peer = pl.ds(pl.multiple_of((1 - core) * half, half), half)
    mine = jnp.where(core == 0, y, x)
    others = jnp.where(core == 0, x, y)
    for cols, axis_at, ref, hbm in ((peer, others, pay, pay_hbm), (own, mine, own_w, None)):
        for d in range(NY):
            i = (axis_at + d) & (NY - 1)
            right = jnp.where(i == NY - 1, 1, 0)
            rows = pl.ds(d * width, width)
            ref[rows, :] = mm(lefts[i], rights[right, :, cols], ((0,), (0,))).astype(ref.dtype)
            if hbm is not None:
                send_out(ref.at[rows], hbm.at[rows])
    for copy in started:
        copy.wait()


def edge_kernel(scalars, senders, receivers, edges, cots, w1, w2, b1, b2, gamma, pieces_s, pieces_r):
    slots, width = edges.shape
    half = width // 2
    share = pieces_s[0].shape[1]
    vmem = pl.BlockSpec(memory_space=pltpu.VMEM)
    hbm = pl.BlockSpec(memory_space=pl.ANY)
    recv_rows = 2 * NY * share
    out_shape = [
        shaped(slots, width),
        shaped(slots, width),
        shaped(NY * width + recv_rows + SMALL, half),
        shaped(NY * width, half, dtype=F32),
        shaped(recv_rows, half, dtype=F32),
        shaped(SMALL, half),
    ]
    return call(
        functools.partial(edge_kernel_body, 1024),
        out_shape,
        [
            senders.reshape(-1, 128),
            receivers.reshape(-1, 128),
            receivers.reshape(1, slots),
            b1.reshape(1, width),
            b2.reshape(1, width),
            gamma.reshape(1, width),
            edges,
            cots,
            w1,
            w2,
            *pieces_s,
            *pieces_r,
        ],
        "edge_step",
        scalars=[scalars],
        where=[vmem] * 6 + [hbm] * 15,
        to=[hbm] * 3 + [vmem] * 3,
        scratch=[
            pltpu.VMEM((NZ, NX, share, width), BF16),
            pltpu.VMEM((NCORE * NY, share, width), BF16),
            pltpu.VMEM((4, slots, width), BF16),
            pltpu.VMEM((slots, width), BF16),
            pltpu.VMEM(w1.shape, BF16),
            pltpu.VMEM(w2.shape, BF16),
            pltpu.VMEM((2, slots, width), BF16),
            pltpu.VMEM((slots, width), BF16),
            pltpu.VMEM(out_shape[2].shape, BF16),
            pltpu.VMEM((slots, 1), jnp.int32),
            pltpu.VMEM((slots, 1), jnp.int32),
            pltpu.SemaphoreType.DMA((15,)),
            pltpu.SemaphoreType.DMA((12,)),
        ],
        flops=10_000_000_000,
        limit=56,
    )


def scatter_body(scalars, send_row, preb, *outs):
    slots, width = preb.shape
    share = outs[0].shape[1]
    grads = preb[...]
    sid_row = send_place(send_row[...], scalars, share)
    for dz, ref in enumerate(outs):
        hit = sid_row == dz * NX * share + lax.broadcasted_iota(jnp.int32, (NX * share, slots), 0)
        ref[...] = mm(one_hot(hit), grads, ((1,), (0,))).astype(BF16).reshape(NX, share, width)


def scatter_kernel(scalars, senders, preb, share):
    slots, width = preb.shape
    out_shape = [shaped(NX, share, width)] * NZ
    args = [senders.reshape(1, slots), preb]
    return call(scatter_body, out_shape, args, "scatter", scalars=[scalars], flops=3_000_000_000, limit=48)


def add_pair(pairs):
    for mine, got, out, first in pairs:
        n, size = got.shape[0], mine.shape[0]
        out[first : first + n] = (mine[first : first + n].astype(F32) + got[...].astype(F32)).astype(BF16)
        if first > 0:
            out[0:first] = mine[0:first]
        if first + n < size:
            out[first + n : size] = mine[first + n : size]


def first_add_body(up, got_up, after, out_up):
    add_pair([(up, got_up, out_up, 0)])


def turn(mine, up, down, keep, sends):
    total = mine[...].astype(F32) + up[...].astype(F32) + down[...].astype(F32)
    keep[...] = total[0]
    for d, ref in enumerate(sends):
        ref[...] = total[d + 1].astype(BF16)


def core_body(own_w, own_r, own_small, got, after, keep, small, keep_r, r_all, *refs):
    sends, (staged, sem) = refs[:3], refs[3:]
    rows, recv = own_w.shape[0] // NY, own_r.shape[0] // NY
    first = own_w.shape[0]
    at = first + own_r.shape[0]
    for d in range(NY):
        total_r = own_r[d * recv : (d + 1) * recv, :] + got[first + d * recv : first + (d + 1) * recv, :].astype(F32)
        if d == 0:
            keep_r[...] = total_r
        else:
            staged[d - 1] = total_r.astype(BF16)
    copy = pltpu.make_async_copy(staged, r_all, sem)
    copy.start()
    summed = split_rows(join_rows(own_small[...]) + join_rows(got[at : at + SMALL, :]))
    small[...] = summed
    for d in range(NY):
        total_w = own_w[d * rows : (d + 1) * rows, :] + got[d * rows : (d + 1) * rows, :].astype(F32)
        if d == 0:
            keep[...] = total_w
        else:
            ref = sends[d - 1]
            ref[0:rows, :] = total_w.astype(BF16)
            ref[rows : rows + SMALL, :] = summed
    copy.wait()


def add_smalls(smalls, own, gots, me, size):
    smalls[me] = own
    for d, got in enumerate(gots):
        smalls[lax.rem(me + size - 1 - d, size)] = got
    total = join_rows(smalls[0])
    for i in range(1, size):
        total = total + join_rows(smalls[i])
    return split_rows(total)


def first_body(place, keep, small, got1, got2, got3, keep_2, small_2, send1, send2, send3, total, smalls):
    me, next_me = place[0], place[1]
    n = keep.shape[0]
    summed = keep[...]
    for got in (got1, got2, got3):
        summed = summed + got[0:n, :].astype(F32)
    total[...] = summed
    small_2[...] = add_smalls(smalls, small[...], [got[n : n + SMALL, :] for got in (got1, got2, got3)], me, NY)
    part = n // NX
    keep_2[...] = total[pl.ds(pl.multiple_of(next_me * part, part), part), :]
    for d, ref in ((1, send1), (2, send2), (3, send3)):
        at = pl.multiple_of(((next_me + d) & (NX - 1)) * part, part)
        ref[0:part, :] = total[pl.ds(at, part), :].astype(BF16)
        ref[part : part + SMALL, :] = small_2[...]


def second_body(
    place, keep, small, got1, got2, got3, up, got_up, down, got_down, r_all, out, out_up, out_down, r1, smalls, sem
):
    copy = pltpu.make_async_copy(r_all.at[0], r1, sem)
    copy.start()
    gots = (got1, got2, got3)
    n = keep.shape[0]
    summed = keep[...]
    for got in gots:
        summed = summed + got[0:n, :].astype(F32)
    out[0:n, :] = summed.astype(BF16)
    out[n : n + SMALL, :] = add_smalls(smalls, small[...], [got[n : n + SMALL, :] for got in gots], place[1], NX)
    add_pair([(up, got_up, out_up, 0), (down, got_down, out_down, 0)])
    copy.wait()


def merge(a, b, out):
    n = a.shape[0] - SMALL
    out[0:n, :] = (a[0:n, :].astype(F32) + b[0:n, :].astype(F32)).astype(BF16)
    out[n : n + SMALL, :] = split_rows(join_rows(a[n : n + SMALL, :]) + join_rows(b[n : n + SMALL, :]))


def merge_body(a, b, r_all, out, r2, sem):
    copy = pltpu.make_async_copy(r_all.at[1], r2, sem)
    copy.start()
    merge(a, b, out)
    copy.wait()


def merge_recv_body(a, b, r_all, keep_r, got_r1, out, r3, total_r, sem):
    copy = pltpu.make_async_copy(r_all.at[2], r3, sem)
    copy.start()
    merge(a, b, out)
    total_r[...] = keep_r[...] + got_r1[...].astype(F32)
    copy.wait()


def last_merge_body(a, b, keep_r, got_r2, got_r3, up, got_up, down, got_down, out, small, total_r, out_up, out_down):
    n = a.shape[0] - SMALL
    out[...] = (a[0:n, :].astype(F32) + b[0:n, :].astype(F32)).astype(BF16)
    small[...] = split_rows(join_rows(a[n : n + SMALL, :]) + join_rows(b[n : n + SMALL, :]))
    total_r[...] = keep_r[...] + got_r2[...].astype(F32) + got_r3[...].astype(F32)
    add_pair([(up, got_up, out_up, 0), (down, got_down, out_down, 0)])


def lay_part_body(place, own, got1, got2, got3, mine, up, down, out, keep, *sends):
    n = own.shape[0]
    for d, ref in enumerate((own, got1, got2, got3)):
        at = pl.multiple_of(((place[1] + d) & (NX - 1)) * n, n)
        out[pl.ds(at, n), :] = ref[...]
    turn(mine, up, down, keep, sends)


def stack_weights_body(own, got1, got2, got3, small, keep, send1, send2, send3, recv, w1, out, grad_nodes):
    n = own.shape[0]
    for d, ref in enumerate((own, got1, got2, got3)):
        out[d * n : (d + 1) * n, :] = ref[...]
    out[NY * n :, :] = small[...]
    nodes(keep, send1, send2, send3, recv, w1, grad_nodes)


def lay_half_body(place, pieces, *refs):
    laid, sems = refs[-2:]
    n, half = laid.shape[1:]
    if len(refs) > 4:
        mine, (grad_w1, grad_w2, *smalls) = refs[2], refs[3:8]
        other = join_rows(pieces[NY * n : NY * n + SMALL, :])
        small = jnp.where(place[1] == 0, other, join_rows(mine[...]))
        for i, ref in enumerate(smalls):
            for h in range(2):
                ref[:, h * half : (h + 1) * half] = small[2 * i + h : 2 * i + h + 1, :]
    else:
        grad_w1, grad_w2 = refs[:2]
    cols = pl.ds(pl.multiple_of(place[1] * half, half), half)
    for d in range(NY):
        i = (place[0] + d) & (NY - 1)
        laid[d] = pieces[d * n : (d + 1) * n, :].astype(F32)

        @pl.when(i < NY - 1)
        def _():
            rows = pl.ds(pl.multiple_of(i * n, n), n)
            pltpu.make_async_copy(laid.at[d], grad_w1.at[rows, cols], sems.at[d]).start()

        @pl.when(i == NY - 1)
        def _():
            pltpu.make_async_copy(laid.at[d], grad_w2.at[:, cols], sems.at[d]).start()

    for d in range(NY):
        pltpu.make_async_copy(laid.at[d], grad_w2.at[:, pl.ds(0, half)], sems.at[d]).wait()


def lay_half(place, pieces, rows, so_far=()):
    half = pieces.shape[1]
    vmem = pl.BlockSpec(memory_space=pltpu.VMEM)
    hbm = pl.BlockSpec(memory_space=pl.ANY)
    out_shape = [shaped((NY - 1) * rows, 2 * half, dtype=F32), shaped(rows, 2 * half, dtype=F32)]
    out_shape += [shaped(1, 2 * half, dtype=F32)] * 3 if so_far else []
    return call(
        lay_half_body,
        out_shape,
        [pieces, *so_far],
        "lay_half",
        scalars=[place],
        where=[vmem] + ([hbm, hbm, vmem] if so_far else []),
        to=[hbm, hbm] + ([vmem] * 3 if so_far else []),
        scratch=[pltpu.VMEM((NY, rows, half), F32), pltpu.SemaphoreType.DMA((NY,))],
        aliases={2: 0, 3: 1} if so_far else {},
    )


def z_ring(up, down):
    return push(up, "z", NZ, 1), push(down, "z", NZ, -1)


def flip(value, bit):
    return lax.ppermute(value, "z", [(i, i ^ bit) for i in range(NZ)])


def reduce_all(place, pay, own_w, own_r, own_small, pieces, w1):
    a0, a1, a2, a3, a4, a5, a6, a7 = pieces
    share, width = a0.shape[1:]
    ring = [shaped(*a0.shape)] * 2
    half = pay.shape[1]
    rows, recv = own_w.shape[0] // NY, own_r.shape[0] // NY
    sum_r, part_r = shaped(recv, half, dtype=F32), shaped(recv, half)
    vmem = pl.BlockSpec(memory_space=pltpu.VMEM)
    hbm = pl.BlockSpec(memory_space=pl.ANY)
    dma = pltpu.SemaphoreType.DMA

    got = push(pay, "core", NCORE, 1)
    got_up = push(a4, "z", NZ, 1)
    out_shape = [shaped(rows, half, dtype=F32), shaped(SMALL, half), sum_r, shaped(3, recv, half)]
    keep, small, keep_r, r_all, *sends = call(
        core_body,
        out_shape + [shaped(rows + SMALL, half)] * 3,
        [own_w, own_r, own_small, got, a4],
        "after_core",
        to=[vmem] * 3 + [hbm] + [vmem] * 3,
        scratch=[pltpu.VMEM((3, recv, half), BF16), dma],
    )
    gots = [swap(part, d + 1, True) for d, part in enumerate(sends)]
    up = call(first_add_body, ring[:1], [a3, got_up, small], "first_add")[0]
    down = a5
    got_up, got_down = z_ring(up, down)

    part = rows // NX
    out_shape = [shaped(part, half, dtype=F32), shaped(SMALL, half)] + [shaped(part + SMALL, half)] * 3
    keep, small, *sends = call(
        first_body,
        out_shape,
        [keep, small, *gots],
        "after_first",
        scalars=[place],
        scratch=[pltpu.VMEM((rows, half), F32), pltpu.VMEM((NY, SMALL, half), BF16)],
    )
    gots = [swap(part, d + 1, False) for d, part in enumerate(sends)]
    payload = shaped(part + SMALL, half)
    value, up, down, r1 = call(
        second_body,
        [payload] + ring + [part_r],
        [keep, small, *gots, a2, got_up, a6, got_down, r_all],
        "after_second",
        scalars=[place],
        where=[vmem] * 9 + [hbm],
        scratch=[pltpu.VMEM((NX, SMALL, half), BF16), dma],
    )
    got_up, got_down = z_ring(up, down)
    got_r1 = push(r1, "y", NY, 1)
    value, r2 = call(
        merge_body, [payload, part_r], [value, flip(value, 1), r_all], "merge_1", where=[vmem] * 2 + [hbm], scratch=[dma]
    )
    got_r2 = push(r2, "y", NY, 2)
    value, r3, keep_r = call(
        merge_recv_body,
        [payload, part_r, sum_r],
        [value, flip(value, 2), r_all, keep_r, got_r1],
        "merge_2",
        where=[vmem] * 2 + [hbm] + [vmem] * 2,
        scratch=[dma],
    )
    got_r3 = push(r3, "y", NY, 3)
    value, small, recv_sum, up, down = call(
        last_merge_body,
        [shaped(part, half), shaped(SMALL, half), sum_r] + ring,
        [value, flip(value, 4), keep_r, got_r2, got_r3, a1, got_up, a7, got_down],
        "merge_4",
    )
    got_up, got_down = z_ring(up, down)
    gots = [swap(value, -d, False) for d in (1, 2, 3)]
    out_shape = [shaped(rows, half), shaped(share, width, dtype=F32)] + [shaped(share, width)] * 3
    value, keep, *sends = call(
        lay_part_body,
        out_shape,
        [value, *gots, a0, got_up, got_down],
        "lay_part",
        scalars=[place],
    )
    gots = [swap(value, -d, True) for d in (1, 2, 3)]
    send_sum = [keep] + [push(part, "x", NX, d + 1) for d, part in enumerate(sends)]
    mine, grad_nodes = call(
        stack_weights_body,
        [shaped(NY * rows + SMALL, half), shaped(share, width, dtype=F32)],
        [value, *gots, small, *send_sum, recv_sum, w1],
        "stack_weights",
        flops=100_000_000,
    )
    other = push(mine, "core", NCORE, 1)
    core = place[2]
    laid = lay_half(jnp.stack([place[0], core]), mine, rows)
    grad_w1, grad_w2, *small = lay_half(jnp.stack([place[1], 1 - core]), other, rows, [*laid, mine[NY * rows :]])
    return grad_w1, grad_w2, [s.reshape(-1) for s in small], grad_nodes


def nodes(keep, got1, got2, got3, recv, w1, out):
    share, width = keep.shape
    half = recv.shape[1]
    total = keep[...] + got1[...].astype(F32) + got2[...].astype(F32) + got3[...].astype(F32)
    total_r = recv[...].astype(BF16)
    out[...] = (
        mm(total.astype(BF16), w1[width : 2 * width, :], ((1,), (1,)))
        + mm(total_r[0:share, :], w1[2 * width :, 0:half], ((1,), (1,)))
        + mm(total_r[share:, :], w1[2 * width :, half:], ((1,), (1,)))
    )


def local(node_latents, edge_latents, cotangent, senders, receivers, edge_count, w1, b1, w2, b2, gamma):
    slots, width = edge_latents.shape[2:]
    share = node_latents.shape[0]
    edges = edge_latents.reshape(slots, width)
    cots = cotangent.reshape(slots, width)
    x, z, y, core = [lax.axis_index(name).astype(jnp.int32) for name in ("x", "z", "y", "core")]
    scalars = jnp.stack([edge_count.reshape(()), core, y, x, z])
    place = jnp.stack([jnp.where(core == 0, y, x), jnp.where(core == 0, x, y), core])

    pieces_s, pieces_r = gather(node_latents)
    grad_edges, preb, pay, own_w, own_r, own_small = edge_kernel(
        scalars, senders, receivers, edges, cots, w1, w2, b1, b2, gamma, pieces_s, pieces_r
    )
    sums = scatter_kernel(scalars, senders, preb, share)
    grad_w1, grad_w2, small, grad_nodes = reduce_all(place, pay, own_w, own_r, own_small, sums, w1)
    return (
        grad_edges.reshape(1, 1, slots, width),
        grad_nodes,
        grad_w1,
        small[0],
        grad_w2,
        small[1],
        small[2],
    )


def solution(mesh):
    mesh = Mesh(mesh.devices.reshape(NX, NZ, NY, NCORE), ("x", "z", "y", "core"))
    row, col = ("x", "z"), ("y", "core")
    in_specs = (
        P(col + row, None),
        P(row, col, None, None),
        P(row, col, None, None),
        P(row, col, None),
        P(row, col, None),
        P(row, col),
        P(),
        P(),
        P(),
        P(),
        P(),
    )
    out_specs = (P(row, col, None, None), P(col + row, None), P(), P(), P(), P(), P())
    return jax.shard_map(local, mesh=mesh, in_specs=in_specs, out_specs=out_specs, check_vma=False)
```
